512 devices in a mesh: lon: 64 (over x, y_hi, z), tp: 8 (over y_lo, core).
Axes of the slice: x: 4, y: 8 (y_hi: 2, y_lo: 4; y = y_hi * 4 + y_lo), z: 8, core: 2. Of those that a mesh axis runs over, the one named last changes fastest.
Arguments:
- qkv: bfloat16 [3, 65536, 2048], P(None, 'lon', 'tp'), may hold values from -5 to 5
- windows: int32 [512, 4], P('lon'), may hold values from 1 to 47, as said below
- out_weight: bfloat16 [2048, 2048], P('tp'), may hold values from -0.125 to 0.125
- cotangent: bfloat16 [65536, 2048], P(('lon', 'tp')), may hold values from -6 to 6
Outputs:
- mixed_rows: bfloat16 [65536, 2048], P(('lon', 'tp'))
- grad_qkv: bfloat16 [3, 65536, 2048], P(None, 'lon', 'tp')
The draws below stay inside these ranges and needn't reach their ends.
Inputs may be any that keep to these rules, and one draw needn't show every extreme that they name: `windows`: for each sector, its 8 rows list 2 x 2 blocks of tiles: tile rows r and (r + 1) mod 16 and tile columns c and c + 1 with c odd, column 2 meaning column 0 of the next sector east (entry 32 + r). r has one parity within a sector. Together the rows cover each such tile exactly once, the sector's column 0 never; rows and the four entries of a row come in any order.
All inputs are finite; a program needn't handle non-finite values.
Results may differ from the reference program's by a relative error of at most 0.017.
Values may be sent and summed in bfloat16 or wider, within the bound.
A program may use at most 64 MiB of HBM per device.

```python
import jax
import jax.numpy as jnp
from jax import lax

D = 2048
HEADS = 16
HEAD_DIM = 128
TILE = 32
LON_TILES = 2
LAT_TILES = 16
TILES = 32
WINDOWS = 8
SECTOR_TOK = 1024
TOKENS = 65536
N_TP = 8


def draw_qkv(key, part):
    key = jax.random.fold_in(key, 5)
    key_base = jax.random.fold_in(key, 0)
    feature_width = HEADS * HEAD_DIM
    shape = (3, TOKENS, feature_width)
    values = jnp.clip(jax.random.normal(key_base, shape, jnp.float32), -5.0, 5.0)
    return values.astype(jnp.bfloat16)


def draw_windows(key, part):
    key = jax.random.fold_in(key, 11)
    key_parity, key_order, key_inner = jax.random.split(key, 3)
    sectors = TOKENS // SECTOR_TOK
    parity = jax.random.randint(key_parity, (sectors, 1), 0, 2)
    window_slot = jnp.arange(WINDOWS)
    band_index = window_slot // (LON_TILES // 2)
    pair_index = window_slot % (LON_TILES // 2)
    top_row = (2 * band_index[None, :] + parity) % LAT_TILES
    bottom = (top_row + 1) % LAT_TILES
    left_col = jnp.broadcast_to((2 * pair_index + 1)[None, :], top_row.shape)
    right_col = left_col + 1

    def tile_index(row_number, col_number):
        return jnp.where(col_number < LON_TILES, row_number * LON_TILES + col_number, TILES + row_number)
    blocks = jnp.stack([tile_index(top_row, left_col), tile_index(top_row, right_col), tile_index(bottom, left_col), tile_index(bottom, right_col)], axis=-1)
    window_order = jax.vmap(lambda sub_key: jax.random.permutation(sub_key, WINDOWS))(jax.random.split(key_order, sectors))
    blocks = jnp.take_along_axis(blocks, window_order[:, :, None], axis=1)
    tile_order = jax.vmap(lambda sub_key: jax.random.permutation(sub_key, 4))(jax.random.split(key_inner, sectors * WINDOWS))
    blocks = jnp.take_along_axis(blocks, tile_order.reshape(sectors, WINDOWS, 4), axis=2)
    return blocks.reshape(sectors * WINDOWS, 4).astype(jnp.int32)


def levels(stream_key, dims, cuts, least, top_value):
    gain, own = 1.0, jax.random.fold_in(stream_key, 6)
    for dim, shards_of in cuts:
        draws = jnp.exp(jax.random.uniform(jax.random.fold_in(own, dim), (shards_of,), jnp.float32, least / len(cuts), top_value / len(cuts)))
        gain = gain * jnp.repeat(draws, dims[dim] // shards_of).reshape([-1 if axis == dim else 1 for axis in range(len(dims))])
    return gain


def bell_draw(stream_key, dims, deviation, most, cuts=(), kind=jnp.bfloat16):
    result = jax.random.normal(stream_key, dims, jnp.float32) * deviation
    if len(cuts) > 0:
        result = levels(stream_key, dims, cuts, -0.22, 0.18) * result
    return jnp.clip(result, min=-most, max=most).astype(kind)


def setup_inputs(seed: int = 0) -> dict:
    arg_keys = jax.random.split(jax.random.key(seed), 5)
    return {
        "qkv": draw_qkv(jax.random.fold_in(arg_keys[4], 71), 0),
        "windows": draw_windows(jax.random.fold_in(arg_keys[4], 71), 0),
        "out_weight": bell_draw(arg_keys[2], (HEADS * HEAD_DIM, D), (HEADS * HEAD_DIM) ** -0.5, 0.125, ((0, 8),)),
        "cotangent": bell_draw(arg_keys[3], (TOKENS, D), 1.0, 6.0, ((0, 512),)),
    }


def window_pass(queries, key_rows, value_rows, grad_out):
    score_scale = HEAD_DIM ** -0.5
    queries_wide = queries.astype(jnp.float32)
    keys_wide = key_rows.astype(jnp.float32)
    values_wide = value_rows.astype(jnp.float32)
    grad_wide = grad_out.astype(jnp.float32)
    scores = jnp.einsum("wqhd,wkhd->whqk", queries_wide, keys_wide) * score_scale
    row_max = jnp.max(scores, axis=-1, keepdims=True)
    raised = jnp.exp(scores - row_max)
    weights = raised / jnp.sum(raised, axis=-1, keepdims=True)
    weights_low = weights.astype(jnp.bfloat16).astype(jnp.float32)
    attended = jnp.einsum("whqk,wkhd->wqhd", weights_low, values_wide).astype(jnp.bfloat16)
    grad_values = jnp.einsum("whqk,wqhd->wkhd", weights_low, grad_wide).astype(jnp.bfloat16)
    grad_weights = jnp.einsum("wqhd,wkhd->whqk", grad_wide, values_wide)
    row_dot = jnp.sum(weights * grad_weights, axis=-1, keepdims=True)
    grad_scores = (weights * (grad_weights - row_dot) * score_scale).astype(jnp.bfloat16).astype(jnp.float32)
    grad_queries = jnp.einsum("whqk,wkhd->wqhd", grad_scores, keys_wide).astype(jnp.bfloat16)
    grad_keys = jnp.einsum("whqk,wqhd->wkhd", grad_scores, queries_wide).astype(jnp.bfloat16)
    return attended, grad_queries, grad_keys, grad_values


def reference(qkv, windows, out_weight, cotangent):
    feature_width = HEADS * HEAD_DIM
    grad_out = jnp.dot(cotangent, out_weight.T, preferred_element_type=jnp.float32).astype(jnp.bfloat16)
    layout = jnp.concatenate([qkv, grad_out[None]], axis=0).reshape(4, TOKENS // TILE, TILE, HEADS, HEAD_DIM)
    sectors = TOKENS // SECTOR_TOK
    sector_of = (jnp.arange(sectors * WINDOWS, dtype=jnp.int32) // WINDOWS)[:, None]
    own_index = sector_of * TILES + windows
    east_index = ((sector_of + 1) % sectors) * TILES + (windows - TILES) * LON_TILES
    tile_list = jnp.where(windows < TILES, own_index, east_index).astype(jnp.int32).reshape(-1)
    gathered = jnp.take(layout, tile_list, axis=1).reshape(4, sectors, WINDOWS, 4 * TILE, HEADS, HEAD_DIM)

    def per_sector(pieces):
        return window_pass(pieces[0], pieces[1], pieces[2], pieces[3])

    results = lax.map(per_sector, jnp.moveaxis(gathered, 1, 0))
    stacked = jnp.stack(results).reshape(4, sectors * WINDOWS * 4, TILE, HEADS, HEAD_DIM)
    placed = jnp.zeros((4, TOKENS // TILE, TILE, HEADS, HEAD_DIM), jnp.bfloat16).at[:, tile_list].set(stacked)
    placed = placed.reshape(4, TOKENS, feature_width)
    attended = placed[0]
    group_width = feature_width // N_TP
    running_sum = jnp.zeros((TOKENS, D), jnp.float32)
    for head_group in range(N_TP):
        low = head_group * group_width
        partial_value = jnp.dot(attended[:, low:low + group_width], out_weight[low:low + group_width],
                          preferred_element_type=jnp.float32).astype(jnp.bfloat16)
        partial_value = lax.optimization_barrier(partial_value)
        running_sum = running_sum + partial_value.astype(jnp.float32)
    return running_sum.astype(jnp.bfloat16), placed[1:]
```

```python
import functools

import jax
import jax.numpy as jnp
from jax import lax
from jax.experimental import pallas as pl
from jax.experimental.pallas import tpu as pltpu
from jax.sharding import PartitionSpec as P

HEAD_DIM = 128
TILE = 32
ROWS = 16
WINDOWS = 8
WIDTH = 256
D = 2048
OWN = 128
HALF = 64
SCALE = HEAD_DIM ** (-0.5)
MESH = pl.DeviceIdType.MESH
BF16 = jnp.bfloat16
F32 = jnp.float32

NT = (((1,), (1,)), ((), ()))
NN = (((1,), (0,)), ((), ()))
TN = (((0,), (0,)), ((), ()))


def dot(a, b, dims):
    return lax.dot_general(a, b, dims, preferred_element_type=F32)


def kernel(
    n_lon,
    mask_ref, qkv_ref, weight_ref, cot_ref,
    mixed_ref, grad_ref,
    west_mask, kv_east, kv_west, gathered, grad_out, q_win, k_win, v_win, do_win,
    weights, out_win, attended, dq_win, dk_own, dv_own, dk_far, dv_far,
    dkv_send, dkv_east, dkv_west, part_out, part_in, part, from_near, from_far,
    lon_send, lon_recv, tp_send, tp_recv, sib_send, sib_recv,
    part_send, part_recv, sum_send, sum_recv,
):
    lon, tp = lax.axis_index("lon"), lax.axis_index("tp")
    chip, core = tp // 2, tp % 2
    east = {"lon": lax.rem(lon + 1, n_lon)}
    west = {"lon": lax.rem(lon + n_lon - 1, n_lon)}
    flip = chip // 2
    pos = chip + flip * (3 - 2 * chip)
    edge, inner = pos == 0, pos == 1

    def chip_at(place):
        return place + flip * (3 - 2 * place)

    def device_at(place, which):
        return 2 * chip_at(place) + which

    near = {"tp": device_at(0, core)}
    one = {"tp": device_at(1, core)}
    far = {"tp": device_at(2, core)}
    sibling = {"tp": 2 * chip + 1 - core}

    barrier = pltpu.get_barrier_semaphore()
    for target in (east, west, sibling):
        pl.semaphore_signal(barrier, inc=1, device_id=target, device_id_type=MESH)

    @pl.when(edge)
    def _():
        pl.semaphore_signal(barrier, inc=1, device_id=one, device_id_type=MESH)
        pl.semaphore_wait(barrier, 4)

    @pl.when(inner)
    def _():
        pl.semaphore_signal(barrier, inc=1, device_id=near, device_id_type=MESH)
        pl.semaphore_signal(barrier, inc=1, device_id=far, device_id_type=MESH)
        pl.semaphore_wait(barrier, 5)

    def remote(src, dst, send_sem, recv_sem, target):
        return pltpu.make_async_remote_copy(
            src_ref=src, dst_ref=dst, send_sem=send_sem, recv_sem=recv_sem,
            device_id=target, device_id_type=MESH,
        )

    pending = []

    def start(copy, condition=None):
        if condition is None:
            copy.start()
        else:
            pl.when(condition)(copy.start)
        pending.append((copy, condition))

    mask_copy = remote(mask_ref, west_mask, lon_send.at[0], lon_recv.at[0], east)
    start(mask_copy)
    to_west = remote(qkv_ref.at[pl.ds(1, 2), :, 0], kv_east, lon_send.at[1], lon_recv.at[1], west)
    to_east = remote(qkv_ref.at[pl.ds(1, 2), :, 1], kv_west, lon_send.at[2], lon_recv.at[2], east)
    start(to_west)
    start(to_east)

    def block(place, which, half):
        return gathered.at[device_at(place, which), half]

    def own_half(half):
        return cot_ref.at[pl.ds(half * HALF, HALF)]

    def slot(place, half):
        return 2 * place + half

    for half in range(2):
        start(remote(own_half(half), gathered.at[tp, half], tp_send.at[half],
                     tp_recv.at[slot(0, half)], one), edge)
        start(remote(own_half(half), gathered.at[tp, half], tp_send.at[half],
                     tp_recv.at[slot(1, half)], near), inner)
        start(remote(own_half(half), gathered.at[tp, half], tp_send.at[2 + half],
                     tp_recv.at[slot(2, half)], far), inner)
        start(remote(own_half(half), gathered.at[tp, half], sib_send.at[half],
                     sib_recv.at[half], sibling))

    def wait_tp(place, half):
        remote(block(place, core, half), block(place, core, half), tp_send.at[0],
               tp_recv.at[slot(place, half)], sibling).wait_recv()

    def hand_over(place, half, order):
        src = block(place, core, half)
        return remote(src, src, sib_send.at[2 * order + half], sib_recv.at[2 * order + half], sibling)

    def gather_step(order, half):
        if order == 1:
            @pl.when(edge)
            def _():
                wait_tp(1, half)
            start(hand_over(1, half, 1), edge)

            @pl.when(inner)
            def _():
                wait_tp(2, half)
            start(remote(block(2, core, half), block(2, core, half), tp_send.at[4 + half],
                         tp_recv.at[slot(2, half)], near), inner)
            start(hand_over(2, half, 1), inner)

            @pl.when(inner)
            def _():
                wait_tp(0, half)
            start(remote(block(0, core, half), block(0, core, half), tp_send.at[6 + half],
                         tp_recv.at[slot(3, half)], far), inner)
            start(hand_over(0, half, 2), inner)
        else:
            place = order
            if order == 2:
                @pl.when(edge)
                def _():
                    wait_tp(2, half)
                start(hand_over(2, half, 2), edge)

                @pl.when(inner)
                def _():
                    wait_tp(3, half)
                start(remote(block(3, core, half), block(3, core, half), tp_send.at[8 + half],
                             tp_recv.at[slot(3, half)], near), inner)
                start(hand_over(3, half, 3), inner)
            else:
                @pl.when(edge)
                def _():
                    wait_tp(3, half)
                start(hand_over(3, half, 3), edge)

    def place_of(order):
        return (pos, 1 + pos, 2 - 2 * pos, 3)[order]

    def wait_hand_over(order):
        for half in range(2):
            dst = gathered.at[device_at(place_of(order), 1 - core), half]
            remote(dst, dst, sib_send.at[0], sib_recv.at[2 * order + half], sibling).wait_recv()

    def project_back(src_rows, device):
        def body(index, carry):
            rows = src_rows(index)
            value = dot(rows, weight_ref[...], NT).astype(BF16)
            grad_out[2 * device + index] = value.reshape(2, TILE, WIDTH)
            return carry
        lax.fori_loop(0, 2, body, 0)

    def project_order(order):
        if order == 0:
            project_back(lambda i: cot_ref[pl.ds(i * HALF, HALF), :], tp)
        else:
            device = device_at(place_of(order), core)
            project_back(lambda i: gathered[device, i], device)
        wait_hand_over(order)
        other = device_at(place_of(order), 1 - core)
        project_back(lambda i: gathered[other, i], other)

    def mask_of(col):
        return (west_mask, mask_ref)[col]

    def into_windows(col, pairs):
        def body(row, carry):
            later = lax.rem(row + 1, ROWS)
            take = mask_of(col)[...] > 0
            for read, write in pairs:
                write(row, jnp.where(take, read(later), read(row)))
            return carry
        lax.fori_loop(0, ROWS, body, 0)

    def from_windows(col, pairs, dtype):
        def body(row, carry):
            before = lax.rem(row + ROWS - 1, ROWS)
            take = mask_of(col)[...].astype(dtype) > 0
            for read, write in pairs:
                write(row, jnp.where(take, read(before), read(row)))
            return carry
        lax.fori_loop(0, ROWS, body, 0)

    def put_query(ref, col):
        def write(row, value):
            ref[col, pl.ds(pl.multiple_of(row * TILE, TILE), TILE), :] = value
        return write

    def put_key(ref, col, remote_half):
        def write(row, value):
            window, part_of = row // 2, row % 2
            place = window * 128 + remote_half * 64 + part_of * TILE
            ref[col, pl.ds(pl.multiple_of(place, TILE), TILE), :] = value
        return write

    def get_window(ref, col):
        return lambda row: ref[col, pl.ds(pl.multiple_of(row * TILE, TILE), TILE), :]

    def own_into_windows(col):
        into_windows(col, [
            (lambda row: qkv_ref[0, row, col], put_query(q_win, col)),
            (lambda row: qkv_ref[1, row, col], put_key(k_win, col, 0)),
            (lambda row: qkv_ref[2, row, col], put_key(v_win, col, 0)),
        ])

    def far_into_windows(col):
        kv = (kv_west, kv_east)[col]
        into_windows(col, [
            (lambda row: kv[0, row], put_key(k_win, col, 1)),
            (lambda row: kv[1, row], put_key(v_win, col, 1)),
        ])

    def forward():
        def body(window, carry):
            qs = pl.ds(pl.multiple_of(window * 64, 64), 64)
            ks = pl.ds(pl.multiple_of(window * 128, 128), 128)
            for col in range(2):
                for head in range(2):
                    lanes = slice(head * HEAD_DIM, (head + 1) * HEAD_DIM)
                    scores = dot(q_win[col, qs, lanes], k_win[col, ks, lanes], NT) * SCALE
                    raised = jnp.exp(scores - jnp.max(scores, axis=-1, keepdims=True))
                    probs = raised / jnp.sum(raised, axis=-1, keepdims=True)
                    weights[col, head, qs, :] = probs
                    out_win[col, qs, lanes] = dot(
                        probs.astype(BF16), v_win[col, ks, lanes], NN
                    ).astype(BF16)
            return carry
        lax.fori_loop(0, WINDOWS, body, 0)

    def backward():
        def body(window, carry):
            qs = pl.ds(pl.multiple_of(window * 64, 64), 64)
            ks = pl.ds(pl.multiple_of(window * 128, 128), 128)
            for col in range(2):
                for head in range(2):
                    lanes = slice(head * HEAD_DIM, (head + 1) * HEAD_DIM)
                    probs = weights[col, head, qs, :]
                    d_out = do_win[col, qs, lanes]
                    grad_w = dot(d_out, v_win[col, ks, lanes], NT)
                    row_dot = jnp.sum(probs * grad_w, axis=-1, keepdims=True)
                    grad_s = (probs * (grad_w - row_dot) * SCALE).astype(BF16)
                    dq_win[col, qs, lanes] = dot(grad_s, k_win[col, ks, lanes], NN).astype(BF16)
                    dk = dot(grad_s, q_win[col, qs, lanes], TN)
                    dv = dot(probs.astype(BF16), d_out, TN)
                    dk_own[col, qs, lanes] = dk[:64]
                    dv_own[col, qs, lanes] = dv[:64]
                    dk_far[col, qs, lanes] = dk[64:].astype(BF16)
                    dv_far[col, qs, lanes] = dv[64:].astype(BF16)
            return carry
        lax.fori_loop(0, WINDOWS, body, 0)

    def project(rows_of, dst):
        rows = attended[pl.ds(2 * rows_of, 2)].reshape(OWN, WIDTH)

        def body(index, carry):
            cols = pl.ds(pl.multiple_of(index * 512, 512), 512)
            value = dot(rows, weight_ref[:, cols], NN).astype(BF16)
            dst[0, :, cols] = value[:HALF]
            dst[1, :, cols] = value[HALF:]
            return carry
        lax.fori_loop(0, D // 512, body, 0)

    def add(total, other):
        def body(index, carry):
            cols = pl.ds(pl.multiple_of(index * 512, 512), 512)
            total[:, cols] = (total[:, cols].astype(F32) + other[:, cols].astype(F32)).astype(BF16)
            return carry
        lax.fori_loop(0, D // 512, body, 0)

    def part_copy(place):
        return remote(part_out.at[place], part_in.at[place], part_send.at[place],
                      part_recv.at[place], sibling)

    def partials(place):
        project(device_at(place, 1 - core), part_out.at[place])
        start(part_copy(place))
        project(device_at(place, core), part.at[place])

    def join_cores(place):
        part_copy(place).wait_recv()
        for half in range(2):
            add(part.at[place, half], part_in.at[place, half])

    def near_sem(place, half):
        return sum_recv.at[2 * (place - 1) + half]

    def far_sem(place, half):
        return sum_recv.at[6 + 2 * place + half]

    def send_edge(place):
        for half in range(2):
            start(remote(part.at[place, half], from_near.at[place - 1, half],
                         sum_send.at[2 * (place - 1) + half], near_sem(place, half), one), edge)

    def wait_near(place, half):
        ref = from_near.at[place - 1, half]
        remote(ref, ref, sum_send.at[0], near_sem(place, half), sibling).wait_recv()

    def wait_far(place, half):
        ref = from_far.at[place, half]
        remote(ref, ref, sum_send.at[0], far_sem(place, half), sibling).wait_recv()

    def pass_far(place, half):
        @pl.when(inner)
        def _():
            wait_near(place, half)
            add(part.at[place, half], from_near.at[place - 1, half])
        start(remote(part.at[place, half], from_far.at[3 - place, half],
                     sum_send.at[2 * (place - 2) + half], far_sem(3 - place, half), far), inner)

    def pass_near(half):
        @pl.when(inner)
        def _():
            wait_far(0, half)
            add(part.at[0, half], from_far.at[0, half])
        start(remote(part.at[0, half], from_far.at[0, half],
                     sum_send.at[4 + half], far_sem(0, half), near), inner)

    project_order(0)
    own_into_windows(1)
    mask_copy.wait_recv()
    own_into_windows(0)
    gather_step(1, 0)
    gather_step(1, 1)
    project_order(1)
    to_west.wait_recv()
    far_into_windows(1)
    to_east.wait_recv()
    far_into_windows(0)
    forward()
    gather_step(2, 0)
    for col in range(2):
        def put_attended(row, value, col=col):
            attended[row, col] = value
        from_windows(col, [(get_window(out_win, col), put_attended)], BF16)
    partials(3)
    partials(2)
    join_cores(3)
    send_edge(3)
    gather_step(2, 1)
    partials(0)
    partials(1)
    join_cores(2)
    send_edge(2)
    join_cores(1)
    send_edge(1)
    join_cores(0)
    project_order(2)
    gather_step(3, 0)
    pass_far(3, 0)
    gather_step(3, 1)
    pass_far(3, 1)
    project_order(3)
    for col in range(2):
        into_windows(col, [(lambda row, col=col: grad_out[row, col], put_query(do_win, col))])
    pass_near(0)
    pass_far(2, 0)
    pass_near(1)
    pass_far(2, 1)
    backward()
    returns = []
    for col in range(2):
        def put_far(which, col=col):
            def write(row, value):
                dkv_send[col, which, row] = value
            return write
        from_windows(col, [(get_window(dk_far, col), put_far(0)), (get_window(dv_far, col), put_far(1))], BF16)
        copy = remote(dkv_send.at[col], (dkv_east, dkv_west)[col], lon_send.at[3 + col],
                      lon_recv.at[3 + col], (west, east)[col])
        start(copy)
        returns.append(copy)
    for col in range(2):
        def put_dq(row, value, col=col):
            grad_ref[0, row, col] = value
        from_windows(col, [(get_window(dq_win, col), put_dq)], BF16)

    def finish(half):
        rows = pl.ds(half * HALF, HALF)

        def body(index, carry):
            cols = pl.ds(pl.multiple_of(index * 512, 512), 512)
            mixed_ref[rows, cols] = (
                part[pos, half, :, cols].astype(F32)
                + from_far[pos, half, :, cols].astype(F32)
                + jnp.where(inner, from_near[0, half, :, cols].astype(F32), 0.0)
            ).astype(BF16)
            return carry
        lax.fori_loop(0, D // 512, body, 0)

    @pl.when(edge)
    def _():
        from_near[0] = jnp.zeros_like(from_near[0])
    for half in range(2):
        @pl.when(inner)
        def _():
            wait_near(1, half)
            wait_far(1, half)

        @pl.when(edge)
        def _():
            wait_far(0, half)
        finish(half)

    for col in range(2):
        returns[1 - col].wait_recv()
        came = (dkv_west, dkv_east)[col]

        def put_sum(which, col=col, came=came):
            def write(row, value):
                grad_ref[1 + which, row, col] = (value + came[which, row].astype(F32)).astype(BF16)
            return write
        from_windows(col, [(get_window(dk_own, col), put_sum(0)), (get_window(dv_own, col), put_sum(1))], F32)

    for copy, condition in pending:
        if condition is None:
            copy.wait_send()
        else:
            pl.when(condition)(copy.wait_send)


def per_device(n_lon, qkv, windows, out_weight, cotangent):
    tile_rows = jnp.where(windows[0] < 2 * ROWS, windows[0] // 2, windows[0] - 2 * ROWS) // 2
    odd = (jnp.max(tile_rows) != jnp.min(tile_rows)).astype(BF16)
    mask = jnp.broadcast_to(odd, (TILE, WIDTH))
    vmem = pl.BlockSpec(memory_space=pltpu.VMEM)
    dma = pltpu.SemaphoreType.DMA
    column = (2, ROWS, TILE, WIDTH)
    mixed, grad = pl.pallas_call(
        functools.partial(kernel, n_lon),
        out_shape=(
            jax.ShapeDtypeStruct((OWN, D), BF16),
            jax.ShapeDtypeStruct((3, ROWS, 2, TILE, WIDTH), BF16),
        ),
        in_specs=[vmem] * 4,
        out_specs=(vmem, vmem),
        scratch_shapes=[
            pltpu.VMEM((TILE, WIDTH), BF16),
            pltpu.VMEM(column, BF16),
            pltpu.VMEM(column, BF16),
            pltpu.VMEM((8, 2, HALF, D), BF16),
            pltpu.VMEM((ROWS, 2, TILE, WIDTH), BF16),
            pltpu.VMEM((2, 512, WIDTH), BF16),
            pltpu.VMEM((2, 1024, WIDTH), BF16),
            pltpu.VMEM((2, 1024, WIDTH), BF16),
            pltpu.VMEM((2, 512, WIDTH), BF16),
            pltpu.VMEM((2, 2, 512, HEAD_DIM), F32),
            pltpu.VMEM((2, 512, WIDTH), BF16),
            pltpu.VMEM((ROWS, 2, TILE, WIDTH), BF16),
            pltpu.VMEM((2, 512, WIDTH), BF16),
            pltpu.VMEM((2, 512, WIDTH), F32),
            pltpu.VMEM((2, 512, WIDTH), F32),
            pltpu.VMEM((2, 512, WIDTH), BF16),
            pltpu.VMEM((2, 512, WIDTH), BF16),
            pltpu.VMEM((2,) + column, BF16),
            pltpu.VMEM(column, BF16),
            pltpu.VMEM(column, BF16),
            pltpu.VMEM((4, 2, HALF, D), BF16),
            pltpu.VMEM((4, 2, HALF, D), BF16),
            pltpu.VMEM((4, 2, HALF, D), BF16),
            pltpu.VMEM((3, 2, HALF, D), BF16),
            pltpu.VMEM((2, 2, HALF, D), BF16),
            dma((5,)), dma((5,)), dma((10,)), dma((8,)), dma((8,)), dma((8,)),
            dma((4,)), dma((4,)), dma((6,)), dma((10,)),
        ],
        compiler_params=pltpu.CompilerParams(
            collective_id=0, has_side_effects=True, vmem_limit_bytes=48 * 1024 * 1024
        ),
        cost_estimate=pl.CostEstimate(
            flops=2 * 1270 * 10**6, bytes_accessed=6 * 2**20, transcendentals=2**18
        ),
    )(mask, qkv.reshape(3, ROWS, 2, TILE, WIDTH), out_weight, cotangent)
    return mixed, grad.reshape(3, ROWS * 2 * TILE, WIDTH)


def solution(mesh):
    in_specs = (P(None, "lon", "tp"), P("lon", None), P("tp", None), P(("lon", "tp"), None))
    out_specs = (P(("lon", "tp"), None), P(None, "lon", "tp"))
    return jax.shard_map(
        functools.partial(per_device, mesh.shape["lon"]),
        mesh=mesh, in_specs=in_specs, out_specs=out_specs, check_vma=False,
    )
```

```python
import functools

import jax
import jax.numpy as jnp
from jax import lax
from jax.experimental import pallas as pl
from jax.experimental.pallas import tpu as pltpu
from jax.sharding import PartitionSpec as P

HEAD_DIM = 128
TILE = 32
ROWS = 16
WINDOWS = 8
WIDTH = 256
D = 2048
OWN = 128
FORWARD_WINDOWS = 2
BACKWARD_WINDOWS = 2
HALF = 64
SCALE = HEAD_DIM ** (-0.5)
MESH = pl.DeviceIdType.MESH
BF16 = jnp.bfloat16
F32 = jnp.float32

NT = (((1,), (1,)), ((), ()))
NN = (((1,), (0,)), ((), ()))
TN = (((0,), (0,)), ((), ()))


def dot(a, b, dims):
    return lax.dot_general(a, b, dims, preferred_element_type=F32)


def kernel(
    n_lon,
    windows_hbm, qkv_hbm, weight_hbm, cot_hbm,
    mixed_ref, grad_ref,
    windows_ref, qkv_ref, weight_ref, mask_ref, west_mask, relay_west, relay_east, kv_east, kv_west, gathered, grad_out, q_win, k_win, v_win, do_win,
    weights, out_win, attended, dq_win, dk_own, dv_own,
    dkv_send, dkv_east, dkv_west, parts, part_in, from_near, from_far,
    load_sem, mask_send, mask_recv, lon_send, lon_recv, piece_send, piece_recv,
    relay_send, relay_recv, tp_send, tp_recv, sib_send, sib_recv,
    part_send, part_recv, sum_send, sum_recv,
):
    lon, tp = lax.axis_index("lon"), lax.axis_index("tp")
    chip, core = tp // 2, tp % 2
    depth = lax.rem(lon, 8)
    first, last = depth == 0, depth == 7
    column_base = lon - depth
    east = {"lon": lax.rem(lon + 1, n_lon)}
    west = {"lon": lax.rem(lon + n_lon - 1, n_lon)}
    over_west = lax.rem(column_base + n_lon - 1, n_lon)
    over_east = lax.rem(column_base + 8, n_lon)
    flip = chip // 2
    pos = chip + flip * (3 - 2 * chip)
    edge, inner = pos == 0, pos == 1

    def chip_at(place):
        return place + flip * (3 - 2 * place)

    def device_at(place, which):
        return 2 * chip_at(place) + which

    near = {"tp": device_at(0, core)}
    one = {"tp": device_at(1, core)}
    far = {"tp": device_at(2, core)}
    sibling = {"tp": 2 * chip + 1 - core}

    loads = [
        pltpu.make_async_copy(src, dst, load_sem.at[index])
        for index, (src, dst) in enumerate((
            (windows_hbm, windows_ref), (cot_hbm, gathered.at[tp]), (weight_hbm, weight_ref), (qkv_hbm, qkv_ref),
        ))
    ]
    for load in loads:
        load.start()

    barrier = pltpu.get_barrier_semaphore()

    def greet(target):
        pl.semaphore_signal(barrier, inc=1, device_id=target, device_id_type=MESH)

    def greet_column(base):
        def body(index, carry):
            greet({"lon": base + index})
            return carry
        lax.fori_loop(0, 8, body, 0)

    greet(sibling)
    pl.when(edge)(lambda: greet(one))

    @pl.when(inner)
    def _():
        greet(near)
        greet(far)

    @pl.when(jnp.logical_not(first))
    def _():
        greet(west)
        greet({"lon": column_base})

    @pl.when(jnp.logical_not(last))
    def _():
        greet(east)
        greet({"lon": column_base + 7})

    pl.when(first)(lambda: greet_column(over_west - 7))
    pl.when(last)(lambda: greet_column(over_east))
    at_end = jnp.logical_or(first, last)
    pl.semaphore_wait(barrier, 2 + jnp.where(inner, 1, 0) + jnp.where(at_end, 10, 4))

    def remote(src, dst, send_sem, recv_sem, target):
        return pltpu.make_async_remote_copy(
            src_ref=src, dst_ref=dst, send_sem=send_sem, recv_sem=recv_sem,
            device_id=target, device_id_type=MESH,
        )

    pending = []

    def start(copy, condition=None):
        if condition is None:
            copy.start()
        else:
            pl.when(condition)(copy.start)
        pending.append((copy, condition))

    def exchange(which, src_west, dst_east, src_east, dst_west, places, rows_from):
        count = len(places)
        stride = 8 // count

        def rows(ref, index):
            return ref.at[:, pl.ds(2 * (rows_from + index), 2)]

        def whole(ref):
            return ref.at[:, pl.ds(2 * rows_from, 2 * count)]

        direct_west = remote(whole(src_west), whole(dst_east), lon_send.at[2 * which],
                             lon_recv.at[2 * which], west)
        direct_east = remote(whole(src_east), whole(dst_west), lon_send.at[2 * which + 1],
                             lon_recv.at[2 * which + 1], east)
        mine = depth // stride
        relays = lax.rem(depth, stride) == places[0]
        sides = ((0, src_west, dst_east, relay_west, first, 0), (1, src_east, dst_west, relay_east, last, 7))

        def over(src, dst, side, condition, index):
            start(remote(src, rows(dst, index), relay_send.at[which, side],
                         piece_recv.at[which, index], {"lon": (over_west, over_east)[side]}), condition)

        def launch():
            for side, src, dst, relay, end, own_place in sides:
                for index, place in sorted(enumerate(places), key=lambda item: abs(item[1] - own_place) % 7):
                    if place == own_place:
                        over(rows(src, index), dst, side, end, index)
                    else:
                        start(remote(rows(src, index), relay.at[which], piece_send.at[which, index],
                                     relay_recv.at[which, side], {"lon": column_base + place}), end)
            start(direct_west, jnp.logical_not(first))
            start(direct_east, jnp.logical_not(last))

        def forward_pieces():
            for side, src, dst, relay, end, own_place in sides:
                condition = jnp.logical_and(relays, jnp.logical_not(end))

                @pl.when(condition)
                def _():
                    remote(relay.at[which], relay.at[which], relay_send.at[which, side],
                           relay_recv.at[which, side], sibling).wait_recv()
                over(relay.at[which], dst, side, condition, mine)

        def wait_from(side):
            copy, dst, at_column_end = ((direct_east, dst_west, first), (direct_west, dst_east, last))[side]
            pl.when(jnp.logical_not(at_column_end))(copy.wait_recv)

            @pl.when(at_column_end)
            def _():
                for index in range(count):
                    remote(rows(dst, index), rows(dst, index), relay_send.at[which, 0],
                           piece_recv.at[which, index], sibling).wait_recv()

        return launch, forward_pieces, wait_from

    send_kv, relay_kv, wait_kv = exchange(
        0, qkv_hbm.at[pl.ds(1, 2), :, 0], kv_east, qkv_hbm.at[pl.ds(1, 2), :, 1], kv_west, list(range(8)), 0
    )
    returns = [
        exchange(1 + stage, dkv_send.at[0], dkv_east, dkv_send.at[1], dkv_west,
                 list(range(stage, 8, 2)), 4 * stage)
        for stage in range(2)
    ]
    send_kv()

    def block(place, which, half):
        return gathered.at[device_at(place, which), half]

    def own_half(half):
        return cot_hbm.at[half]

    def slot(place, half):
        return 2 * place + half

    for half in range(2):
        start(remote(own_half(half), gathered.at[tp, half], tp_send.at[half],
                     tp_recv.at[slot(0, half)], one), edge)
        start(remote(own_half(half), gathered.at[tp, half], tp_send.at[half],
                     tp_recv.at[slot(1, half)], near), inner)
        start(remote(own_half(half), gathered.at[tp, half], tp_send.at[2 + half],
                     tp_recv.at[slot(2, half)], far), inner)
        start(remote(own_half(half), gathered.at[tp, half], sib_send.at[half],
                     sib_recv.at[half], sibling))

    def wait_tp(place, half):
        remote(block(place, core, half), block(place, core, half), tp_send.at[0],
               tp_recv.at[slot(place, half)], sibling).wait_recv()

    def hand_over(place, half, order):
        src = block(place, core, half)
        return remote(src, src, sib_send.at[2 * order + half], sib_recv.at[2 * order + half], sibling)

    def gather_step(order, half):
        if order == 1:
            @pl.when(edge)
            def _():
                wait_tp(1, half)
            start(hand_over(1, half, 1), edge)

            @pl.when(inner)
            def _():
                wait_tp(2, half)
            start(remote(block(2, core, half), block(2, core, half), tp_send.at[4 + half],
                         tp_recv.at[slot(2, half)], near), inner)
            start(hand_over(2, half, 1), inner)

            @pl.when(inner)
            def _():
                wait_tp(0, half)
            start(remote(block(0, core, half), block(0, core, half), tp_send.at[6 + half],
                         tp_recv.at[slot(3, half)], far), inner)
            start(hand_over(0, half, 2), inner)
        else:
            place = order
            if order == 2:
                @pl.when(edge)
                def _():
                    wait_tp(2, half)
                start(hand_over(2, half, 2), edge)

                @pl.when(inner)
                def _():
                    wait_tp(3, half)
                start(remote(block(3, core, half), block(3, core, half), tp_send.at[8 + half],
                             tp_recv.at[slot(3, half)], near), inner)
                start(hand_over(3, half, 3), inner)
            else:
                @pl.when(edge)
                def _():
                    wait_tp(3, half)
                start(hand_over(3, half, 3), edge)

    def place_of(order):
        return (pos, 1 + pos, 2 - 2 * pos, 3)[order]

    def wait_hand_over(order):
        for half in range(2):
            dst = gathered.at[device_at(place_of(order), 1 - core), half]
            remote(dst, dst, sib_send.at[0], sib_recv.at[2 * order + half], sibling).wait_recv()

    def project_back(order):
        source = chip_at(place_of(order))
        rows = gathered[pl.ds(2 * source, 2)].reshape(2 * OWN, D)
        value = dot(rows, weight_ref[...], NT).astype(BF16)
        grad_out[pl.ds(4 * source, 4)] = value.reshape(4, 2, TILE, WIDTH)

    def project_order(order):
        wait_hand_over(order)
        project_back(order)

    def mask_of(col):
        return (west_mask, mask_ref)[col]

    def into_windows(col, pairs):
        def body(row, carry):
            later = lax.rem(row + 1, ROWS)
            take = mask_of(col)[...] > 0
            for read, write in pairs:
                write(row, jnp.where(take, read(later), read(row)))
            return carry
        lax.fori_loop(0, ROWS, body, 0)

    def from_windows(col, pairs, dtype):
        def body(row, carry):
            before = lax.rem(row + ROWS - 1, ROWS)
            take = mask_of(col)[...].astype(dtype) > 0
            for read, write in pairs:
                write(row, jnp.where(take, read(before), read(row)))
            return carry
        lax.fori_loop(0, ROWS, body, 0)

    def put_query(ref, col):
        def write(row, value):
            ref[col, pl.ds(pl.multiple_of(row * TILE, TILE), TILE), :] = value
        return write

    def put_key(ref, col, remote_half):
        def write(row, value):
            window, part_of = row // 2, row % 2
            place = window * 128 + remote_half * 64 + part_of * TILE
            ref[col, pl.ds(pl.multiple_of(place, TILE), TILE), :] = value
        return write

    def get_window(ref, col):
        return lambda row: ref[col, pl.ds(pl.multiple_of(row * TILE, TILE), TILE), :]

    def own_into_windows(col):
        into_windows(col, [
            (lambda row: qkv_ref[0, row, col], put_query(q_win, col)),
            (lambda row: qkv_ref[1, row, col], put_key(k_win, col, 0)),
            (lambda row: qkv_ref[2, row, col], put_key(v_win, col, 0)),
        ])

    def far_into_windows(col):
        kv = (kv_west, kv_east)[col]
        into_windows(col, [
            (lambda row: kv[0, row], put_key(k_win, col, 1)),
            (lambda row: kv[1, row], put_key(v_win, col, 1)),
        ])

    UNITS = [(col, head) for col in range(2) for head in range(2)]

    def unit(ref, col, head, place):
        return ref[col, place, head * HEAD_DIM:(head + 1) * HEAD_DIM]

    def forward():
        def body(step, carry):
            spots = []
            for sub in range(FORWARD_WINDOWS):
                window = step * FORWARD_WINDOWS + sub
                qs = pl.ds(pl.multiple_of(window * 64, 64), 64)
                ks = pl.ds(pl.multiple_of(window * 128, 128), 128)
                spots += [(col, head, qs, ks) for col, head in UNITS]
            values = [unit(v_win, col, head, ks) for col, head, qs, ks in spots]
            scores = [
                dot(unit(q_win, col, head, qs), unit(k_win, col, head, ks), NT) * SCALE
                for col, head, qs, ks in spots
            ]
            raised = [jnp.exp(x - jnp.max(x, axis=-1, keepdims=True)) for x in scores]
            probs = [x / jnp.sum(x, axis=-1, keepdims=True) for x in raised]
            outs = [dot(x.astype(BF16), v, NN).astype(BF16) for x, v in zip(probs, values)]
            for (col, head, qs, ks), x, out in zip(spots, probs, outs):
                weights[col, head, qs, :] = x
                out_win[col, qs, head * HEAD_DIM:(head + 1) * HEAD_DIM] = out
            return carry
        lax.fori_loop(0, WINDOWS // FORWARD_WINDOWS, body, 0)

    def backward(stage):
        def body(step, carry):
            spots = []
            for sub in range(BACKWARD_WINDOWS):
                slot_at = stage * 4 + step * BACKWARD_WINDOWS + sub
                window = lax.rem(slot_at + 3 * flip, WINDOWS)
                qs = pl.ds(pl.multiple_of(window * 64, 64), 64)
                ks = pl.ds(pl.multiple_of(window * 128, 128), 128)
                spots += [(col, head, qs, ks, slot_at) for col, head in UNITS]
            queries = [unit(q_win, col, head, qs) for col, head, qs, ks, _ in spots]
            keys = [unit(k_win, col, head, ks) for col, head, qs, ks, _ in spots]
            d_outs = [unit(do_win, col, head, qs) for col, head, qs, ks, _ in spots]
            probs = [weights[col, head, qs, :] for col, head, qs, ks, _ in spots]
            grad_w = [
                dot(d, unit(v_win, col, head, ks), NT) for d, (col, head, qs, ks, _) in zip(d_outs, spots)
            ]
            dvs = [dot(x.astype(BF16), d, TN) for x, d in zip(probs, d_outs)]
            row_dots = [jnp.sum(x * g, axis=-1, keepdims=True) for x, g in zip(probs, grad_w)]
            grad_s = [(x * (g - r) * SCALE).astype(BF16) for x, g, r in zip(probs, grad_w, row_dots)]
            dqs = [dot(g, k, NN).astype(BF16) for g, k in zip(grad_s, keys)]
            dks = [dot(g, q, TN) for g, q in zip(grad_s, queries)]
            for (col, head, qs, ks, slot_at), dq, dk, dv in zip(spots, dqs, dks, dvs):
                lanes = slice(head * HEAD_DIM, (head + 1) * HEAD_DIM)
                dq_win[col, qs, lanes] = dq
                dk_own[col, qs, lanes] = dk[:64]
                dv_own[col, qs, lanes] = dv[:64]
                dkv_send[col, 0, pl.ds(2 * slot_at, 2), :, lanes] = dk[64:].astype(BF16).reshape(2, TILE, HEAD_DIM)
                dkv_send[col, 1, pl.ds(2 * slot_at, 2), :, lanes] = dv[64:].astype(BF16).reshape(2, TILE, HEAD_DIM)
            return carry
        lax.fori_loop(0, 4 // BACKWARD_WINDOWS, body, 0)

    def project(place):
        rows = attended[pl.ds(4 * chip_at(place), 4)].reshape(2 * OWN, WIDTH)

        def body(index, carry):
            cols = pl.ds(pl.multiple_of(index * 512, 512), 512)
            value = dot(rows, weight_ref[:, cols], NN).astype(BF16)
            parts[place, :, :, :, cols] = value.reshape(2, 2, HALF, 512)
            return carry
        lax.fori_loop(0, D // 512, body, 0)

    def add(total, other):
        def body(index, carry):
            cols = pl.ds(pl.multiple_of(index * 512, 512), 512)
            total[:, cols] = (total[:, cols].astype(F32) + other[:, cols].astype(F32)).astype(BF16)
            return carry
        lax.fori_loop(0, D // 512, body, 0)

    def part(place, half):
        return parts.at[place, core, half]

    def part_copy(place):
        return remote(parts.at[place, 1 - core], part_in.at[place], part_send.at[place],
                      part_recv.at[place], sibling)

    def partials(place):
        project(place)
        start(part_copy(place))

    def join_cores(place):
        part_copy(place).wait_recv()
        for half in range(2):
            add(part(place, half), part_in.at[place, half])

    def near_sem(place, half):
        return sum_recv.at[2 * (place - 1) + half]

    def far_sem(place, half):
        return sum_recv.at[6 + 2 * place + half]

    def send_edge(place):
        for half in range(2):
            start(remote(part(place, half), from_near.at[place - 1, half],
                         sum_send.at[2 * (place - 1) + half], near_sem(place, half), one), edge)

    def wait_near(place, half):
        ref = from_near.at[place - 1, half]
        remote(ref, ref, sum_send.at[0], near_sem(place, half), sibling).wait_recv()

    def wait_far(place, half):
        ref = from_far.at[place, half]
        remote(ref, ref, sum_send.at[0], far_sem(place, half), sibling).wait_recv()

    def pass_far(place, half):
        @pl.when(inner)
        def _():
            wait_near(place, half)
            add(part(place, half), from_near.at[place - 1, half])
        start(remote(part(place, half), from_far.at[3 - place, half],
                     sum_send.at[2 * (place - 2) + half], far_sem(3 - place, half), far), inner)

    def pass_near(half):
        @pl.when(inner)
        def _():
            wait_far(0, half)
            add(part(0, half), from_far.at[0, half])
        start(remote(part(0, half), from_far.at[0, half],
                     sum_send.at[4 + half], far_sem(0, half), near), inner)

    loads[0].wait()
    tiles = windows_ref[...]
    tile_rows = jnp.where(tiles < 2 * ROWS, tiles // 4, (tiles - 2 * ROWS) // 2)
    odd = jnp.max(tile_rows, axis=0, keepdims=True) != jnp.min(tile_rows, axis=0, keepdims=True)
    mask_ref[...] = jnp.broadcast_to(odd[:, :1].astype(F32), (TILE, WIDTH)).astype(BF16)
    mask_copy = remote(mask_ref, west_mask, mask_send.at[0], mask_recv.at[0], east)
    start(mask_copy)
    for load in loads[1:]:
        load.wait()
    own_into_windows(1)
    project_order(0)
    relay_kv()
    mask_copy.wait_recv()
    own_into_windows(0)
    gather_step(1, 0)
    gather_step(1, 1)
    project_order(1)
    wait_kv(1)
    far_into_windows(1)
    wait_kv(0)
    far_into_windows(0)
    forward()
    gather_step(2, 0)
    for col in range(2):
        def put_attended(row, value, col=col):
            attended[row, col] = value
        from_windows(col, [(get_window(out_win, col), put_attended)], BF16)
    partials(3)
    partials(2)
    partials(0)
    join_cores(3)
    send_edge(3)
    partials(1)
    join_cores(2)
    send_edge(2)
    gather_step(2, 1)
    join_cores(1)
    send_edge(1)
    join_cores(0)

    def grad_out_into_windows():
        for col in range(2):
            into_windows(col, [(lambda row, col=col: grad_out[row, col], put_query(do_win, col))])

    project_order(2)
    grad_out_into_windows()
    backward(0)
    returns[0][0]()
    pass_far(3, 0)
    gather_step(3, 0)
    pass_far(3, 1)
    gather_step(3, 1)
    returns[0][1]()
    project_order(3)
    grad_out_into_windows()
    backward(1)
    returns[1][0]()
    pass_near(0)
    pass_far(2, 0)
    pass_near(1)
    pass_far(2, 1)
    returns[1][1]()
    for col in range(2):
        def put_dq(row, value, col=col):
            grad_ref[0, row, col] = value
        from_windows(col, [(get_window(dq_win, col), put_dq)], BF16)

    def finish(half):
        rows = pl.ds(half * HALF, HALF)

        def body(index, carry):
            cols = pl.ds(pl.multiple_of(index * 512, 512), 512)
            mixed_ref[rows, cols] = (
                parts[pos, core, half, :, cols].astype(F32)
                + from_far[pos, half, :, cols].astype(F32)
                + jnp.where(inner, from_near[0, half, :, cols].astype(F32), 0.0)
            ).astype(BF16)
            return carry
        lax.fori_loop(0, D // 512, body, 0)

    @pl.when(edge)
    def _():
        from_near[0] = jnp.zeros_like(from_near[0])
    for half in range(2):
        @pl.when(inner)
        def _():
            wait_near(1, half)
            wait_far(1, half)

        @pl.when(edge)
        def _():
            wait_far(0, half)
        finish(half)

    for col in range(2):
        for stage in range(2):
            returns[stage][2](col)
        came = (dkv_west, dkv_east)[col]

        def put_sum(which, col=col):
            def write(row, value):
                grad_ref[1 + which, row, col] = value.astype(BF16)
            return write

        def get_sum(which, ref, col=col, came=came):
            own = get_window(ref, col)
            return lambda row: own(row) + came[which, lax.rem(row + 10 * flip, ROWS)].astype(F32)

        from_windows(col, [(get_sum(0, dk_own), put_sum(0)), (get_sum(1, dv_own), put_sum(1))], F32)

    for copy, condition in pending:
        if condition is None:
            copy.wait_send()
        else:
            pl.when(condition)(copy.wait_send)


def per_device(n_lon, qkv, windows, out_weight, cotangent):
    vmem = pl.BlockSpec(memory_space=pltpu.VMEM)
    anywhere = pl.BlockSpec(memory_space=pl.ANY)
    dma = pltpu.SemaphoreType.DMA
    column = (2, ROWS, TILE, WIDTH)
    mixed, grad = pl.pallas_call(
        functools.partial(kernel, n_lon),
        out_shape=(
            jax.ShapeDtypeStruct((OWN, D), BF16),
            jax.ShapeDtypeStruct((3, ROWS, 2, TILE, WIDTH), BF16),
        ),
        in_specs=[anywhere] * 4,
        out_specs=(vmem, vmem),
        scratch_shapes=[
            pltpu.VMEM((4, WINDOWS), jnp.int32),
            pltpu.VMEM((3, ROWS, 2, TILE, WIDTH), BF16),
            pltpu.VMEM((WIDTH, D), BF16),
            pltpu.VMEM((TILE, WIDTH), BF16),
            pltpu.VMEM((TILE, WIDTH), BF16),
            pltpu.VMEM((3, 2, 2, TILE, WIDTH), BF16),
            pltpu.VMEM((3, 2, 2, TILE, WIDTH), BF16),
            pltpu.VMEM(column, BF16),
            pltpu.VMEM(column, BF16),
            pltpu.VMEM((8, 2, HALF, D), BF16),
            pltpu.VMEM((ROWS, 2, TILE, WIDTH), BF16),
            pltpu.VMEM((2, 512, WIDTH), BF16),
            pltpu.VMEM((2, 1024, WIDTH), BF16),
            pltpu.VMEM((2, 1024, WIDTH), BF16),
            pltpu.VMEM((2, 512, WIDTH), BF16),
            pltpu.VMEM((2, 2, 512, HEAD_DIM), F32),
            pltpu.VMEM((2, 512, WIDTH), BF16),
            pltpu.VMEM((ROWS, 2, TILE, WIDTH), BF16),
            pltpu.VMEM((2, 512, WIDTH), BF16),
            pltpu.VMEM((2, 512, WIDTH), F32),
            pltpu.VMEM((2, 512, WIDTH), F32),
            pltpu.VMEM((2,) + column, BF16),
            pltpu.VMEM(column, BF16),
            pltpu.VMEM(column, BF16),
            pltpu.VMEM((4, 2, 2, HALF, D), BF16),
            pltpu.VMEM((4, 2, HALF, D), BF16),
            pltpu.VMEM((3, 2, HALF, D), BF16),
            pltpu.VMEM((2, 2, HALF, D), BF16),
            dma((4,)), dma((1,)), dma((1,)), dma((6,)), dma((6,)), dma((3, 8)), dma((3, 8)),
            dma((3, 2)), dma((3, 2)), dma((10,)), dma((8,)), dma((8,)), dma((8,)),
            dma((4,)), dma((4,)), dma((6,)), dma((10,)),
        ],
        compiler_params=pltpu.CompilerParams(
            collective_id=0, has_side_effects=True, vmem_limit_bytes=56 * 1024 * 1024
        ),
        cost_estimate=pl.CostEstimate(
            flops=2 * 1270 * 10**6, bytes_accessed=6 * 2**20, transcendentals=2**18
        ),
    )(windows.T, qkv.reshape(3, ROWS, 2, TILE, WIDTH), out_weight, cotangent.reshape(2, HALF, D))
    return mixed, grad.reshape(3, ROWS * 2 * TILE, WIDTH)


def solution(mesh):
    in_specs = (P(None, "lon", "tp"), P("lon", None), P("tp", None), P(("lon", "tp"), None))
    out_specs = (P(("lon", "tp"), None), P(None, "lon", "tp"))
    return jax.shard_map(
        functools.partial(per_device, mesh.shape["lon"]),
        mesh=mesh, in_specs=in_specs, out_specs=out_specs, check_vma=False,
    )
```

```python
import functools

import jax
import jax.numpy as jnp
from jax import lax
from jax.experimental import pallas as pl
from jax.experimental.pallas import tpu as pltpu
from jax.sharding import PartitionSpec as P

HEAD_DIM = 128
TILE = 32
ROWS = 16
WINDOWS = 8
WIDTH = 256
D = 2048
OWN = 128
ORDER = (4, 3, 5, 2, 6, 1, 7, 0)
BACKWARD_WINDOWS = 2
HALF = 64
SCALE = HEAD_DIM ** (-0.5)
MESH = pl.DeviceIdType.MESH
BF16 = jnp.bfloat16
F32 = jnp.float32

NT = (((1,), (1,)), ((), ()))
NN = (((1,), (0,)), ((), ()))
TN = (((0,), (0,)), ((), ()))


def dot(a, b, dims):
    return lax.dot_general(a, b, dims, preferred_element_type=F32)


def kernel(
    n_lon,
    windows_hbm, qkv_hbm, weight_hbm, cot_hbm,
    mixed_ref, grad_ref,
    windows_ref, qkv_ref, weight_ref, mask_ref, west_mask, relay_west, relay_east, kv_east, kv_west, gathered, grad_out, q_win, k_win, v_win, do_win,
    weights, out_win, attended, dq_win, dk_own, dv_own,
    dkv_send, dkv_east, dkv_west, parts, part_in, from_near, from_far,
    load_sem, mask_send, mask_recv, lon_send, lon_recv, piece_send, piece_recv,
    relay_send, relay_recv, tp_send, tp_recv, sib_send, sib_recv,
    part_send, part_recv, sum_send, sum_recv,
):
    lon, tp = lax.axis_index("lon"), lax.axis_index("tp")
    chip, core = tp // 2, tp % 2
    depth = lax.rem(lon, 8)
    first, last = depth == 0, depth == 7
    column_base = lon - depth
    east = {"lon": lax.rem(lon + 1, n_lon)}
    west = {"lon": lax.rem(lon + n_lon - 1, n_lon)}
    over_west = lax.rem(column_base + n_lon - 1, n_lon)
    over_east = lax.rem(column_base + 8, n_lon)
    flip = chip // 2
    pos = chip + flip * (3 - 2 * chip)
    edge, inner = pos == 0, pos == 1
    edge_chip, inner_chip = edge, inner

    def chip_at(place):
        return place + flip * (3 - 2 * place)

    def device_at(place, which):
        return 2 * chip_at(place) + which

    near = {"tp": device_at(0, core)}
    one = {"tp": device_at(1, core)}
    far = {"tp": device_at(2, core)}
    sibling = {"tp": 2 * chip + 1 - core}

    loads = [
        pltpu.make_async_copy(src, dst, load_sem.at[index])
        for index, (src, dst) in enumerate((
            (windows_hbm, windows_ref), (cot_hbm, gathered.at[tp]), (weight_hbm, weight_ref), (qkv_hbm, qkv_ref),
        ))
    ]
    for load in loads:
        load.start()

    barrier = pltpu.get_barrier_semaphore()

    def greet(target):
        pl.semaphore_signal(barrier, inc=1, device_id=target, device_id_type=MESH)

    def greet_column(base):
        def body(index, carry):
            greet({"lon": base + index})
            return carry
        lax.fori_loop(0, 8, body, 0)

    greet(sibling)
    pl.when(edge)(lambda: greet(one))

    @pl.when(inner)
    def _():
        greet(near)
        greet(far)

    @pl.when(jnp.logical_not(first))
    def _():
        greet(west)
        greet({"lon": column_base})

    @pl.when(jnp.logical_not(last))
    def _():
        greet(east)
        greet({"lon": column_base + 7})

    pl.when(first)(lambda: greet_column(over_west - 7))
    pl.when(last)(lambda: greet_column(over_east))
    at_end = jnp.logical_or(first, last)
    pl.semaphore_wait(barrier, 2 + jnp.where(inner, 1, 0) + jnp.where(at_end, 10, 4))

    def remote(src, dst, send_sem, recv_sem, target):
        return pltpu.make_async_remote_copy(
            src_ref=src, dst_ref=dst, send_sem=send_sem, recv_sem=recv_sem,
            device_id=target, device_id_type=MESH,
        )

    pending = []

    def start(copy, condition=None):
        if condition is None:
            copy.start()
        else:
            pl.when(condition)(copy.start)
        pending.append((copy, condition))

    def exchange(which, src_west, dst_east, src_east, dst_west, row_of, runs):
        count = 8

        def rows(ref, index):
            return ref.at[:, pl.ds(row_of(index), 1)]

        def direct(src, dst, side, target):
            return [
                remote(src.at[:, pl.ds(begin, length)], dst.at[:, pl.ds(begin, length)],
                       lon_send.at[which, side, run], lon_recv.at[which, side, run], target)
                for run, (begin, length) in enumerate(runs)
            ]

        direct_west = direct(src_west, dst_east, 0, west)
        direct_east = direct(src_east, dst_west, 1, east)

        sides = ((0, src_west, dst_east, relay_west, first, 0), (1, src_east, dst_west, relay_east, last, 7))

        def over(src, dst, side, condition, index):
            start(remote(src, rows(dst, index), relay_send.at[which, side],
                         piece_recv.at[which, index], {"lon": (over_west, over_east)[side]}), condition)

        def launch():
            for side, src, dst, relay, end, own_place in sides:
                for step in ORDER:
                    place = abs(own_place - step)
                    if step == 0:
                        over(rows(src, place), dst, side, end, place)
                    else:
                        start(remote(rows(src, place), relay.at[which], piece_send.at[which, place],
                                     relay_recv.at[which, side], {"lon": column_base + place}), end)
            for copy in direct_west:
                start(copy, jnp.logical_not(first))
            for copy in direct_east:
                start(copy, jnp.logical_not(last))

        def forward_pieces():
            for side, src, dst, relay, end, own_place in sides:
                condition = jnp.logical_not(end)

                @pl.when(condition)
                def _():
                    remote(relay.at[which], relay.at[which], relay_send.at[which, side],
                           relay_recv.at[which, side], sibling).wait_recv()
                over(relay.at[which], dst, side, condition, depth)

        def wait_from(side):
            copies, dst, at_column_end = ((direct_east, dst_west, first), (direct_west, dst_east, last))[side]

            @pl.when(jnp.logical_not(at_column_end))
            def _():
                for copy in copies:
                    copy.wait_recv()

            @pl.when(at_column_end)
            def _():
                for index in range(count):
                    remote(rows(dst, index), rows(dst, index), relay_send.at[which, 0],
                           piece_recv.at[which, index], sibling).wait_recv()

        return launch, forward_pieces, wait_from

    def first_row(index):
        return jnp.where(index < 6, 10 - 10 * flip + index, 14 * flip + index - 6)

    def second_row(index):
        return 2 + 4 * flip + index

    kv_halves = [
        exchange(half, qkv_hbm.at[pl.ds(1, 2), :, 0], kv_east, qkv_hbm.at[pl.ds(1, 2), :, 1], kv_west, row_of, runs)
        for half, (row_of, runs) in enumerate((
            (first_row, [(10 - 10 * flip, 6), (14 * flip, 2)]),
            (second_row, [(2 + 4 * flip, 8)]),
        ))
    ]
    returns = [
        exchange(2 + stage, dkv_send.at[0], dkv_east, dkv_send.at[1], dkv_west,
                 lambda index, stage=stage: 8 * stage + index, [(8 * stage, 8)])
        for stage in range(2)
    ]
    kv_halves[0][0]()
    kv_halves[1][0]()

    def block(place, which, half):
        return gathered.at[device_at(place, which), half]

    def own_half(half):
        return cot_hbm.at[half]

    def slot(place, half):
        return 2 * place + half

    for half in range(2):
        start(remote(own_half(half), gathered.at[tp, half], tp_send.at[half],
                     tp_recv.at[slot(0, half)], one), edge)
        start(remote(own_half(half), gathered.at[tp, half], tp_send.at[half],
                     tp_recv.at[slot(1, half)], near), inner)
        start(remote(own_half(half), gathered.at[tp, half], tp_send.at[2 + half],
                     tp_recv.at[slot(2, half)], far), inner)
        start(remote(own_half(half), gathered.at[tp, half], sib_send.at[half],
                     sib_recv.at[half], sibling))

    def wait_tp(place, half):
        remote(block(place, core, half), block(place, core, half), tp_send.at[0],
               tp_recv.at[slot(place, half)], sibling).wait_recv()

    def hand_over(place, half, order):
        src = block(place, core, half)
        return remote(src, src, sib_send.at[2 * order + half], sib_recv.at[2 * order + half], sibling)

    def gather_step(order, half, where=None):
        def both(condition):
            return condition if where is None else jnp.logical_and(condition, where)

        edge, inner = both(edge_chip), both(inner_chip)
        if order == 1:
            @pl.when(edge)
            def _():
                wait_tp(1, half)
            start(hand_over(1, half, 1), edge)

            @pl.when(inner)
            def _():
                wait_tp(2, half)
            start(remote(block(2, core, half), block(2, core, half), tp_send.at[4 + half],
                         tp_recv.at[slot(2, half)], near), inner)
            start(hand_over(2, half, 1), inner)

            @pl.when(inner)
            def _():
                wait_tp(0, half)
            start(remote(block(0, core, half), block(0, core, half), tp_send.at[6 + half],
                         tp_recv.at[slot(3, half)], far), inner)
            start(hand_over(0, half, 2), inner)
        else:
            place = order
            if order == 2:
                @pl.when(edge)
                def _():
                    wait_tp(2, half)
                start(hand_over(2, half, 2), edge)

                @pl.when(inner)
                def _():
                    wait_tp(3, half)
                start(remote(block(3, core, half), block(3, core, half), tp_send.at[8 + half],
                             tp_recv.at[slot(3, half)], near), inner)
                start(hand_over(3, half, 3), inner)
            else:
                @pl.when(edge)
                def _():
                    wait_tp(3, half)
                start(hand_over(3, half, 3), edge)

    def place_of(order):
        return (pos, 1 + pos, 2 - 2 * pos, 3)[order]

    def wait_hand_over(order):
        for half in range(2):
            dst = gathered.at[device_at(place_of(order), 1 - core), half]
            remote(dst, dst, sib_send.at[0], sib_recv.at[2 * order + half], sibling).wait_recv()

    def project_back(order):
        source = chip_at(place_of(order))
        rows = gathered[pl.ds(2 * source, 2)].reshape(2 * OWN, D)
        value = dot(rows, weight_ref[...], NT).astype(BF16)
        grad_out[pl.ds(4 * source, 4)] = value.reshape(4, 2, TILE, WIDTH)

    def project_order(order):
        wait_hand_over(order)
        project_back(order)

    def mask_of(col):
        return (west_mask, mask_ref)[col]

    def into_windows(col, pairs, begin=0, count=ROWS):
        def body(index, carry):
            row = lax.rem(begin + index, ROWS)
            later = lax.rem(row + 1, ROWS)
            take = mask_of(col)[...] > 0
            for read, write in pairs:
                write(row, jnp.where(take, read(later), read(row)))
            return carry
        lax.fori_loop(0, count, body, 0)

    def from_windows(col, pairs, dtype, begin=0, count=ROWS):
        def body(index, carry):
            row = lax.rem(begin + index, ROWS)
            before = lax.rem(row + ROWS - 1, ROWS)
            take = mask_of(col)[...].astype(dtype) > 0
            for read, write in pairs:
                write(row, jnp.where(take, read(before), read(row)))
            return carry
        lax.fori_loop(0, count, body, 0)

    def put_query(ref, col):
        def write(row, value):
            ref[col, pl.ds(pl.multiple_of(row * TILE, TILE), TILE), :] = value
        return write

    def put_key(ref, col, remote_half):
        def write(row, value):
            window, part_of = row // 2, row % 2
            place = window * 128 + remote_half * 64 + part_of * TILE
            ref[col, pl.ds(pl.multiple_of(place, TILE), TILE), :] = value
        return write

    def get_window(ref, col):
        return lambda row: ref[col, pl.ds(pl.multiple_of(row * TILE, TILE), TILE), :]

    def own_into_windows(col):
        into_windows(col, [
            (lambda row: qkv_ref[0, row, col], put_query(q_win, col)),
            (lambda row: qkv_ref[1, row, col], put_key(k_win, col, 0)),
            (lambda row: qkv_ref[2, row, col], put_key(v_win, col, 0)),
        ])

    def far_into_windows(col, begin, count):
        kv = (kv_west, kv_east)[col]
        into_windows(col, [
            (lambda row: kv[0, row], put_key(k_win, col, 1)),
            (lambda row: kv[1, row], put_key(v_win, col, 1)),
        ], 2 * begin, 2 * count)

    UNITS = [(col, head) for col in range(2) for head in range(2)]

    def unit(ref, col, head, place):
        return ref[col, place, head * HEAD_DIM:(head + 1) * HEAD_DIM]

    def forward(begin, count):
        spots = []
        for sub in range(count):
            window = lax.rem(begin + sub, WINDOWS)
            qs = pl.ds(pl.multiple_of(window * 64, 64), 64)
            ks = pl.ds(pl.multiple_of(window * 128, 128), 128)
            spots += [(col, head, qs, ks) for col, head in UNITS]
        values = [unit(v_win, col, head, ks) for col, head, qs, ks in spots]
        scores = [
            dot(unit(q_win, col, head, qs), unit(k_win, col, head, ks), NT) * SCALE
            for col, head, qs, ks in spots
        ]
        raised = [jnp.exp(x - jnp.max(x, axis=-1, keepdims=True)) for x in scores]
        probs = [x / jnp.sum(x, axis=-1, keepdims=True) for x in raised]
        outs = [dot(x.astype(BF16), v, NN).astype(BF16) for x, v in zip(probs, values)]
        for (col, head, qs, ks), x, out in zip(spots, probs, outs):
            weights[col, head, qs, :] = x
            out_win[col, qs, head * HEAD_DIM:(head + 1) * HEAD_DIM] = out

    def attend(begin, count):
        for col in range(2):
            def put_attended(row, value, col=col):
                attended[row, col] = value
            from_windows(col, [(get_window(out_win, col), put_attended)], BF16, begin, count)

    def backward(stage):
        def body(step, carry):
            spots = []
            for sub in range(BACKWARD_WINDOWS):
                slot_at = stage * 4 + step * BACKWARD_WINDOWS + sub
                window = lax.rem(slot_at + 3 * flip, WINDOWS)
                qs = pl.ds(pl.multiple_of(window * 64, 64), 64)
                ks = pl.ds(pl.multiple_of(window * 128, 128), 128)
                spots += [(col, head, qs, ks, slot_at) for col, head in UNITS]
            queries = [unit(q_win, col, head, qs) for col, head, qs, ks, _ in spots]
            keys = [unit(k_win, col, head, ks) for col, head, qs, ks, _ in spots]
            d_outs = [unit(do_win, col, head, qs) for col, head, qs, ks, _ in spots]
            probs = [weights[col, head, qs, :] for col, head, qs, ks, _ in spots]
            grad_w = [
                dot(d, unit(v_win, col, head, ks), NT) for d, (col, head, qs, ks, _) in zip(d_outs, spots)
            ]
            dvs = [dot(x.astype(BF16), d, TN) for x, d in zip(probs, d_outs)]
            row_dots = [jnp.sum(x * g, axis=-1, keepdims=True) for x, g in zip(probs, grad_w)]
            grad_s = [(x * (g - r) * SCALE).astype(BF16) for x, g, r in zip(probs, grad_w, row_dots)]
            dqs = [dot(g, k, NN).astype(BF16) for g, k in zip(grad_s, keys)]
            dks = [dot(g, q, TN) for g, q in zip(grad_s, queries)]
            for (col, head, qs, ks, slot_at), dq, dk, dv in zip(spots, dqs, dks, dvs):
                lanes = slice(head * HEAD_DIM, (head + 1) * HEAD_DIM)
                dq_win[col, qs, lanes] = dq
                dk_own[col, qs, lanes] = dk[:64]
                dv_own[col, qs, lanes] = dv[:64]
                dkv_send[col, 0, pl.ds(2 * slot_at, 2), :, lanes] = dk[64:].astype(BF16).reshape(2, TILE, HEAD_DIM)
                dkv_send[col, 1, pl.ds(2 * slot_at, 2), :, lanes] = dv[64:].astype(BF16).reshape(2, TILE, HEAD_DIM)
            return carry
        lax.fori_loop(0, 4 // BACKWARD_WINDOWS, body, 0)

    def project(place):
        rows = attended[pl.ds(4 * chip_at(place), 4)].reshape(2 * OWN, WIDTH)

        def body(index, carry):
            cols = pl.ds(pl.multiple_of(index * 512, 512), 512)
            value = dot(rows, weight_ref[:, cols], NN).astype(BF16)
            parts[place, :, :, :, cols] = value.reshape(2, 2, HALF, 512)
            return carry
        lax.fori_loop(0, D // 512, body, 0)

    def add(total, other):
        def body(index, carry):
            cols = pl.ds(pl.multiple_of(index * 512, 512), 512)
            total[:, cols] = (total[:, cols].astype(F32) + other[:, cols].astype(F32)).astype(BF16)
            return carry
        lax.fori_loop(0, D // 512, body, 0)

    def part(place, half):
        return parts.at[place, core, half]

    def part_copy(place):
        return remote(parts.at[place, 1 - core], part_in.at[place], part_send.at[place],
                      part_recv.at[place], sibling)

    def partials(place):
        project(place)
        start(part_copy(place))

    def join_cores(place):
        part_copy(place).wait_recv()
        for half in range(2):
            add(part(place, half), part_in.at[place, half])

    def near_sem(place, half):
        return sum_recv.at[2 * (place - 1) + half]

    def far_sem(place, half):
        return sum_recv.at[6 + 2 * place + half]

    def send_edge(place):
        for half in range(2):
            start(remote(part(place, half), from_near.at[place - 1, half],
                         sum_send.at[2 * (place - 1) + half], near_sem(place, half), one), edge)

    def wait_near(place, half):
        ref = from_near.at[place - 1, half]
        remote(ref, ref, sum_send.at[0], near_sem(place, half), sibling).wait_recv()

    def wait_far(place, half):
        ref = from_far.at[place, half]
        remote(ref, ref, sum_send.at[0], far_sem(place, half), sibling).wait_recv()

    def pass_far(place, half):
        @pl.when(inner)
        def _():
            wait_near(place, half)
            add(part(place, half), from_near.at[place - 1, half])
        start(remote(part(place, half), from_far.at[3 - place, half],
                     sum_send.at[2 * (place - 2) + half], far_sem(3 - place, half), far), inner)

    def pass_near(half):
        @pl.when(inner)
        def _():
            wait_far(0, half)
            add(part(0, half), from_far.at[0, half])
        start(remote(part(0, half), from_far.at[0, half],
                     sum_send.at[4 + half], far_sem(0, half), near), inner)

    loads[0].wait()
    tiles = windows_ref[...]
    tile_rows = jnp.where(tiles < 2 * ROWS, tiles // 4, (tiles - 2 * ROWS) // 2)
    odd = jnp.max(tile_rows, axis=0, keepdims=True) != jnp.min(tile_rows, axis=0, keepdims=True)
    mask_ref[...] = jnp.broadcast_to(odd[:, :1].astype(F32), (TILE, WIDTH)).astype(BF16)
    mask_copy = remote(mask_ref, west_mask, mask_send.at[0], mask_recv.at[0], east)
    start(mask_copy)
    for load in loads[1:]:
        load.wait()
    own_into_windows(1)
    kv_halves[0][1]()
    mask_copy.wait_recv()
    own_into_windows(0)
    kv_halves[1][1]()
    inside = jnp.logical_not(at_end)
    gather_step(1, 0)
    gather_step(1, 1, at_end)
    near_window = 5 + 2 * flip
    for col in (1, 0):
        kv_halves[0][2](col)
        far_into_windows(col, near_window, 3)
    forward(near_window, 3)
    attend(4 * chip_at(3), 4)
    partials(3)
    gather_step(1, 1, inside)
    join_cores(3)
    send_edge(3)
    project_order(0)
    project_order(1)
    gather_step(2, 0, at_end)
    for col in (1, 0):
        kv_halves[1][2](col)
        far_into_windows(col, near_window + 3, 5)
    forward(near_window + 3, 3)
    forward(near_window + 6, 2)
    attend(4 * chip_at(3) + 4, 12)
    gather_step(2, 0, inside)
    partials(2)
    partials(0)
    partials(1)
    join_cores(2)
    send_edge(2)
    pass_far(3, 0)
    join_cores(1)
    send_edge(1)
    join_cores(0)
    gather_step(2, 1)
    pass_far(3, 1)

    def grad_out_into_windows():
        for col in range(2):
            into_windows(col, [(lambda row, col=col: grad_out[row, col], put_query(do_win, col))])

    project_order(2)
    grad_out_into_windows()
    backward(0)
    returns[0][0]()
    gather_step(3, 0)
    pass_near(0)
    gather_step(3, 1)
    pass_far(2, 0)
    project_order(3)
    grad_out_into_windows()
    backward(1)
    returns[1][0]()
    returns[0][1]()
    pass_near(1)
    pass_far(2, 1)
    returns[1][1]()
    for col in range(2):
        def put_dq(row, value, col=col):
            grad_ref[0, row, col] = value
        from_windows(col, [(get_window(dq_win, col), put_dq)], BF16)

    def finish(half):
        rows = pl.ds(half * HALF, HALF)

        def body(index, carry):
            cols = pl.ds(pl.multiple_of(index * 512, 512), 512)
            mixed_ref[rows, cols] = (
                parts[pos, core, half, :, cols].astype(F32)
                + from_far[pos, half, :, cols].astype(F32)
                + jnp.where(inner, from_near[0, half, :, cols].astype(F32), 0.0)
            ).astype(BF16)
            return carry
        lax.fori_loop(0, D // 512, body, 0)

    @pl.when(edge)
    def _():
        from_near[0] = jnp.zeros_like(from_near[0])
    for half in range(2):
        @pl.when(inner)
        def _():
            wait_near(1, half)
            wait_far(1, half)

        @pl.when(edge)
        def _():
            wait_far(0, half)
        finish(half)

    for col in range(2):
        for stage in range(2):
            returns[stage][2](col)
        came = (dkv_west, dkv_east)[col]

        def put_sum(which, col=col):
            def write(row, value):
                grad_ref[1 + which, row, col] = value.astype(BF16)
            return write

        def get_sum(which, ref, col=col, came=came):
            own = get_window(ref, col)
            return lambda row: own(row) + came[which, lax.rem(row + 10 * flip, ROWS)].astype(F32)

        from_windows(col, [(get_sum(0, dk_own), put_sum(0)), (get_sum(1, dv_own), put_sum(1))], F32)

    for copy, condition in pending:
        if condition is None:
            copy.wait_send()
        else:
            pl.when(condition)(copy.wait_send)


def per_device(n_lon, qkv, windows, out_weight, cotangent):
    vmem = pl.BlockSpec(memory_space=pltpu.VMEM)
    dma = pltpu.SemaphoreType.DMA
    column = (2, ROWS, TILE, WIDTH)
    mixed, grad = pl.pallas_call(
        functools.partial(kernel, n_lon),
        out_shape=(
            jax.ShapeDtypeStruct((OWN, D), BF16),
            jax.ShapeDtypeStruct((3, ROWS, 2, TILE, WIDTH), BF16),
        ),
        in_specs=[pl.BlockSpec(memory_space=pltpu.HBM)] * 4,
        out_specs=(vmem, vmem),
        scratch_shapes=[
            pltpu.VMEM((4, WINDOWS), jnp.int32),
            pltpu.VMEM((3, ROWS, 2, TILE, WIDTH), BF16),
            pltpu.VMEM((WIDTH, D), BF16),
            pltpu.VMEM((TILE, WIDTH), BF16),
            pltpu.VMEM((TILE, WIDTH), BF16),
            pltpu.VMEM((4, 2, 1, TILE, WIDTH), BF16),
            pltpu.VMEM((4, 2, 1, TILE, WIDTH), BF16),
            pltpu.VMEM(column, BF16),
            pltpu.VMEM(column, BF16),
            pltpu.VMEM((8, 2, HALF, D), BF16),
            pltpu.VMEM((ROWS, 2, TILE, WIDTH), BF16),
            pltpu.VMEM((2, 512, WIDTH), BF16),
            pltpu.VMEM((2, 1024, WIDTH), BF16),
            pltpu.VMEM((2, 1024, WIDTH), BF16),
            pltpu.VMEM((2, 512, WIDTH), BF16),
            pltpu.VMEM((2, 2, 512, HEAD_DIM), F32),
            pltpu.VMEM((2, 512, WIDTH), BF16),
            pltpu.VMEM((ROWS, 2, TILE, WIDTH), BF16),
            pltpu.VMEM((2, 512, WIDTH), BF16),
            pltpu.VMEM((2, 512, WIDTH), F32),
            pltpu.VMEM((2, 512, WIDTH), F32),
            pltpu.VMEM((2,) + column, BF16),
            pltpu.VMEM(column, BF16),
            pltpu.VMEM(column, BF16),
            pltpu.VMEM((4, 2, 2, HALF, D), BF16),
            pltpu.VMEM((4, 2, HALF, D), BF16),
            pltpu.VMEM((3, 2, HALF, D), BF16),
            pltpu.VMEM((2, 2, HALF, D), BF16),
            dma((4,)), dma((1,)), dma((1,)), dma((4, 2, 2)), dma((4, 2, 2)), dma((4, 8)), dma((4, 8)),
            dma((4, 2)), dma((4, 2)), dma((10,)), dma((8,)), dma((8,)), dma((8,)),
            dma((4,)), dma((4,)), dma((6,)), dma((10,)),
        ],
        compiler_params=pltpu.CompilerParams(
            collective_id=0, has_side_effects=True, vmem_limit_bytes=53 * 1024 * 1024
        ),
        cost_estimate=pl.CostEstimate(
            flops=2 * 1270 * 10**6, bytes_accessed=6 * 2**20, transcendentals=2**18
        ),
    )(windows.T, qkv.reshape(3, ROWS, 2, TILE, WIDTH), out_weight, cotangent.reshape(2, HALF, D))
    return mixed, grad.reshape(3, ROWS * 2 * TILE, WIDTH)


def solution(mesh):
    in_specs = (P(None, "lon", "tp"), P("lon", None), P("tp", None), P(("lon", "tp"), None))
    out_specs = (P(("lon", "tp"), None), P(None, "lon", "tp"))
    return jax.shard_map(
        functools.partial(per_device, mesh.shape["lon"]),
        mesh=mesh, in_specs=in_specs, out_specs=out_specs, check_vma=False,
    )
```

```python
import functools

import jax
import jax.numpy as jnp
from jax import lax
from jax.experimental import pallas as pl
from jax.experimental.pallas import tpu as pltpu
from jax.sharding import PartitionSpec as P

HEAD_DIM = 128
TILE = 32
ROWS = 16
WINDOWS = 8
WIDTH = 256
D = 2048
OWN = 128
ORDER = (4, 3, 5, 2, 6, 1, 7, 0)
HALF = 64
SCALE = HEAD_DIM ** (-0.5)
MESH = pl.DeviceIdType.MESH
BF16 = jnp.bfloat16
F32 = jnp.float32

NT = (((1,), (1,)), ((), ()))
NN = (((1,), (0,)), ((), ()))
TN = (((0,), (0,)), ((), ()))


def dot(a, b, dims):
    return lax.dot_general(a, b, dims, preferred_element_type=F32)


def kernel(
    n_lon,
    windows_hbm, qkv_hbm, weight_hbm, cot_hbm,
    mixed_ref, grad_ref,
    windows_ref, qkv_ref, weight_ref, mask_ref, west_mask, relay_west, relay_east, kv_east, kv_west, gathered, grad_out, q_win, k_win, v_win, do_win,
    weights, out_win, attended, dq_win, dk_own, dv_own,
    dkv_send, dkv_east, dkv_west, parts, part_in, from_near, from_far,
    load_sem, mask_send, mask_recv, lon_send, lon_recv, piece_send, piece_recv,
    relay_send, relay_recv, tp_send, tp_recv, sib_send, sib_recv,
    part_send, part_recv, sum_send, sum_recv,
):
    lon, tp = lax.axis_index("lon"), lax.axis_index("tp")
    chip, core = tp // 2, tp % 2
    depth = lax.rem(lon, 8)
    first, last = depth == 0, depth == 7
    column_base = lon - depth
    east = {"lon": lax.rem(lon + 1, n_lon)}
    west = {"lon": lax.rem(lon + n_lon - 1, n_lon)}
    over_west = lax.rem(column_base + n_lon - 1, n_lon)
    over_east = lax.rem(column_base + 8, n_lon)
    flip = chip // 2
    pos = chip + flip * (3 - 2 * chip)
    edge, inner = pos == 0, pos == 1
    edge_chip, inner_chip = edge, inner

    def chip_at(place):
        return place + flip * (3 - 2 * place)

    def device_at(place, which):
        return 2 * chip_at(place) + which

    near = {"tp": device_at(0, core)}
    one = {"tp": device_at(1, core)}
    far = {"tp": device_at(2, core)}
    sibling = {"tp": 2 * chip + 1 - core}

    loads = [
        pltpu.make_async_copy(src, dst, load_sem.at[index])
        for index, (src, dst) in enumerate((
            (windows_hbm, windows_ref), (cot_hbm, gathered.at[tp]), (weight_hbm, weight_ref), (qkv_hbm, qkv_ref),
        ))
    ]
    for load in loads:
        load.start()

    barrier = pltpu.get_barrier_semaphore()

    def greet(target):
        pl.semaphore_signal(barrier, inc=1, device_id=target, device_id_type=MESH)

    def greet_column(base):
        def body(index, carry):
            greet({"lon": base + index})
            return carry
        lax.fori_loop(0, 8, body, 0)

    greet(sibling)
    pl.when(edge)(lambda: greet(one))

    @pl.when(inner)
    def _():
        greet(near)
        greet(far)

    @pl.when(jnp.logical_not(first))
    def _():
        greet(west)
        greet({"lon": column_base})

    @pl.when(jnp.logical_not(last))
    def _():
        greet(east)
        greet({"lon": column_base + 7})

    pl.when(first)(lambda: greet_column(over_west - 7))
    pl.when(last)(lambda: greet_column(over_east))
    at_end = jnp.logical_or(first, last)
    pl.semaphore_wait(barrier, 2 + jnp.where(inner, 1, 0) + jnp.where(at_end, 10, 4))

    def remote(src, dst, send_sem, recv_sem, target):
        return pltpu.make_async_remote_copy(
            src_ref=src, dst_ref=dst, send_sem=send_sem, recv_sem=recv_sem,
            device_id=target, device_id_type=MESH,
        )

    pending = []

    def start(copy, condition=None):
        if condition is None:
            copy.start()
        else:
            pl.when(condition)(copy.start)
        pending.append((copy, condition))

    def exchange(which, src_west, dst_east, src_east, dst_west, shares, runs):
        def rows(ref, share, place):
            return ref.at[:, pl.ds(share[2](place), share[1])]

        def direct(src, dst, side, target):
            return [
                remote(src.at[:, pl.ds(begin, length)], dst.at[:, pl.ds(begin, length)],
                       lon_send.at[which, side, run], lon_recv.at[which, side, run], target)
                for run, (begin, length) in enumerate(runs)
            ]

        direct_west = direct(src_west, dst_east, 0, west)
        direct_east = direct(src_east, dst_west, 1, east)

        sides = ((0, src_west, dst_east, relay_west, first, 0), (1, src_east, dst_west, relay_east, last, 7))

        def over(src, dst, side, condition, share, place):
            start(remote(src, rows(dst, share, place), relay_send.at[which, side],
                         piece_recv.at[which, place], {"lon": (over_west, over_east)[side]}), condition)

        def passing(relay, share):
            return relay.at[which, :, pl.ds(0, share[1])]

        def launch():
            for side, src, dst, relay, end, own_place in sides:
                for step in ORDER:
                    place = abs(own_place - step)
                    share = next((item for item in shares if place in item[0]), None)
                    if share is None:
                        continue
                    if step == 0:
                        over(rows(src, share, place), dst, side, end, share, place)
                    else:
                        start(remote(rows(src, share, place), passing(relay, share), piece_send.at[which, place],
                                     relay_recv.at[which, side], {"lon": column_base + place}), end)
            for copy in direct_west:
                start(copy, jnp.logical_not(first))
            for copy in direct_east:
                start(copy, jnp.logical_not(last))

        def forward_pieces():
            for side, src, dst, relay, end, own_place in sides:
                for share in shares:
                    among = functools.reduce(jnp.logical_or, [depth == place for place in share[0]])
                    condition = jnp.logical_and(among, jnp.logical_not(end))
                    piece = passing(relay, share)

                    @pl.when(condition)
                    def _():
                        remote(piece, piece, relay_send.at[which, side],
                               relay_recv.at[which, side], sibling).wait_recv()
                    over(piece, dst, side, condition, share, depth)

        def wait_from(side):
            copies, dst, at_column_end = ((direct_east, dst_west, first), (direct_west, dst_east, last))[side]

            @pl.when(jnp.logical_not(at_column_end))
            def _():
                for copy in copies:
                    copy.wait_recv()

            @pl.when(at_column_end)
            def _():
                for share in shares:
                    for place in share[0]:
                        ref = rows(dst, share, place)
                        remote(ref, ref, relay_send.at[which, 0], piece_recv.at[which, place], sibling).wait_recv()

        return launch, forward_pieces, wait_from

    def first_row(index):
        return jnp.where(index < 6, 10 - 10 * flip + index, 14 * flip + index - 6)

    def second_row(index):
        return 2 + 4 * flip + index

    kv_halves = [
        exchange(half, qkv_hbm.at[pl.ds(1, 2), :, 0], kv_east, qkv_hbm.at[pl.ds(1, 2), :, 1], kv_west,
                 [(range(8), 1, row_of)], runs)
        for half, (row_of, runs) in enumerate((
            (first_row, [(10 - 10 * flip, 6), (14 * flip, 2)]),
            (second_row, [(2 + 4 * flip, 8)]),
        ))
    ]
    return_shares = (
        [((0, 7), 2, lambda place: 2 * (place // 7)), (range(1, 7), 1, lambda place: 3 + place)],
        [((0, 1, 2, 5, 6, 7), 1, lambda place: 10 + place - 2 * (place // 5))],
    )
    returns = [
        exchange(2 + stage, dkv_send.at[0], dkv_east, dkv_send.at[1], dkv_west, return_shares[stage], [run])
        for stage, run in enumerate(((0, 10), (10, 6)))
    ]
    kv_halves[0][0]()

    def block(place, which, half):
        return gathered.at[device_at(place, which), half]

    def own_half(half):
        return cot_hbm.at[half]

    def slot(place, half):
        return 2 * place + half

    def send_own(half):
        start(remote(own_half(half), gathered.at[tp, half], tp_send.at[half],
                     tp_recv.at[slot(0, half)], one), edge)
        start(remote(own_half(half), gathered.at[tp, half], tp_send.at[half],
                     tp_recv.at[slot(1, half)], near), inner)
        start(remote(own_half(half), gathered.at[tp, half], tp_send.at[2 + half],
                     tp_recv.at[slot(2, half)], far), inner)
        start(remote(own_half(half), gathered.at[tp, half], sib_send.at[half],
                     sib_recv.at[half], sibling))

    send_own(0)

    def wait_tp(place, half):
        remote(block(place, core, half), block(place, core, half), tp_send.at[0],
               tp_recv.at[slot(place, half)], sibling).wait_recv()

    def hand_over(place, half, order):
        src = block(place, core, half)
        return remote(src, src, sib_send.at[2 * order + half], sib_recv.at[2 * order + half], sibling)

    def gather_step(order, half, where=None):
        def both(condition):
            return condition if where is None else jnp.logical_and(condition, where)

        edge, inner = both(edge_chip), both(inner_chip)
        if order == 1:
            @pl.when(edge)
            def _():
                wait_tp(1, half)
            start(hand_over(1, half, 1), edge)

            @pl.when(inner)
            def _():
                wait_tp(2, half)
            start(remote(block(2, core, half), block(2, core, half), tp_send.at[4 + half],
                         tp_recv.at[slot(2, half)], near), inner)
            start(hand_over(2, half, 1), inner)

            @pl.when(inner)
            def _():
                wait_tp(0, half)
            start(remote(block(0, core, half), block(0, core, half), tp_send.at[6 + half],
                         tp_recv.at[slot(3, half)], far), inner)
            start(hand_over(0, half, 2), inner)
        else:
            place = order
            if order == 2:
                @pl.when(edge)
                def _():
                    wait_tp(2, half)
                start(hand_over(2, half, 2), edge)

                @pl.when(inner)
                def _():
                    wait_tp(3, half)
                start(remote(block(3, core, half), block(3, core, half), tp_send.at[8 + half],
                             tp_recv.at[slot(3, half)], near), inner)
                start(hand_over(3, half, 3), inner)
            else:
                @pl.when(edge)
                def _():
                    wait_tp(3, half)
                start(hand_over(3, half, 3), edge)

    def place_of(order):
        return (pos, 1 + pos, 2 - 2 * pos, 3)[order]

    def wait_hand_over(order):
        for half in range(2):
            dst = gathered.at[device_at(place_of(order), 1 - core), half]
            remote(dst, dst, sib_send.at[0], sib_recv.at[2 * order + half], sibling).wait_recv()

    def project_back(order):
        source = chip_at(place_of(order))
        rows = gathered[pl.ds(2 * source, 2)].reshape(2 * OWN, D)
        value = dot(rows, weight_ref[...], NT).astype(BF16)
        grad_out[pl.ds(4 * source, 4)] = value.reshape(4, 2, TILE, WIDTH)

    def project_order(order):
        wait_hand_over(order)
        project_back(order)

    def mask_of(col):
        return (west_mask, mask_ref)[col]

    def into_windows(col, pairs, begin=0, count=ROWS):
        def body(index, carry):
            row = lax.rem(begin + index, ROWS)
            later = lax.rem(row + 1, ROWS)
            take = mask_of(col)[...] > 0
            for read, write in pairs:
                write(row, jnp.where(take, read(later), read(row)))
            return carry
        lax.fori_loop(0, count, body, 0)

    def from_windows(col, pairs, dtype, begin=0, count=ROWS):
        def body(index, carry):
            row = lax.rem(begin + index, ROWS)
            before = lax.rem(row + ROWS - 1, ROWS)
            take = mask_of(col)[...].astype(dtype) > 0
            for read, write in pairs:
                write(row, jnp.where(take, read(before), read(row)))
            return carry
        lax.fori_loop(0, count, body, 0)

    def put_query(ref, col):
        def write(row, value):
            ref[col, pl.ds(pl.multiple_of(row * TILE, TILE), TILE), :] = value
        return write

    def put_key(ref, col, remote_half):
        def write(row, value):
            window, part_of = row // 2, row % 2
            place = window * 128 + remote_half * 64 + part_of * TILE
            ref[col, pl.ds(pl.multiple_of(place, TILE), TILE), :] = value
        return write

    def get_window(ref, col):
        return lambda row: ref[col, pl.ds(pl.multiple_of(row * TILE, TILE), TILE), :]

    def own_into_windows(col):
        into_windows(col, [
            (lambda row: qkv_ref[0, row, col], put_query(q_win, col)),
            (lambda row: qkv_ref[1, row, col], put_key(k_win, col, 0)),
            (lambda row: qkv_ref[2, row, col], put_key(v_win, col, 0)),
        ])

    def far_into_windows(col, begin, count):
        kv = (kv_west, kv_east)[col]
        into_windows(col, [
            (lambda row: kv[0, row], put_key(k_win, col, 1)),
            (lambda row: kv[1, row], put_key(v_win, col, 1)),
        ], 2 * begin, 2 * count)

    UNITS = [(col, head) for col in range(2) for head in range(2)]

    def unit(ref, col, head, place):
        return ref[col, place, head * HEAD_DIM:(head + 1) * HEAD_DIM]

    def forward(begin, count):
        spots = []
        for sub in range(count):
            window = lax.rem(begin + sub, WINDOWS)
            qs = pl.ds(pl.multiple_of(window * 64, 64), 64)
            ks = pl.ds(pl.multiple_of(window * 128, 128), 128)
            spots += [(col, head, qs, ks) for col, head in UNITS]
        values = [unit(v_win, col, head, ks) for col, head, qs, ks in spots]
        scores = [
            dot(unit(q_win, col, head, qs), unit(k_win, col, head, ks), NT) * SCALE
            for col, head, qs, ks in spots
        ]
        raised = [jnp.exp(x - jnp.max(x, axis=-1, keepdims=True)) for x in scores]
        probs = [x / jnp.sum(x, axis=-1, keepdims=True) for x in raised]
        outs = [dot(x.astype(BF16), v, NN).astype(BF16) for x, v in zip(probs, values)]
        for (col, head, qs, ks), x, out in zip(spots, probs, outs):
            weights[col, head, qs, :] = x
            out_win[col, qs, head * HEAD_DIM:(head + 1) * HEAD_DIM] = out

    def attend(begin, count):
        for col in range(2):
            def put_attended(row, value, col=col):
                attended[row, col] = value
            from_windows(col, [(get_window(out_win, col), put_attended)], BF16, begin, count)

    def backward(begin, count):
        spots = []
        for sub in range(count):
            slot_at = begin + sub
            window = lax.rem(slot_at + 2 * flip, WINDOWS)
            qs = pl.ds(pl.multiple_of(window * 64, 64), 64)
            ks = pl.ds(pl.multiple_of(window * 128, 128), 128)
            spots += [(col, head, qs, ks, slot_at) for col, head in UNITS]
        queries = [unit(q_win, col, head, qs) for col, head, qs, ks, _ in spots]
        keys = [unit(k_win, col, head, ks) for col, head, qs, ks, _ in spots]
        d_outs = [unit(do_win, col, head, qs) for col, head, qs, ks, _ in spots]
        probs = [weights[col, head, qs, :] for col, head, qs, ks, _ in spots]
        grad_w = [
            dot(d, unit(v_win, col, head, ks), NT) for d, (col, head, qs, ks, _) in zip(d_outs, spots)
        ]
        dvs = [dot(x.astype(BF16), d, TN) for x, d in zip(probs, d_outs)]
        row_dots = [jnp.sum(x * g, axis=-1, keepdims=True) for x, g in zip(probs, grad_w)]
        grad_s = [(x * (g - r) * SCALE).astype(BF16) for x, g, r in zip(probs, grad_w, row_dots)]
        dqs = [dot(g, k, NN).astype(BF16) for g, k in zip(grad_s, keys)]
        dks = [dot(g, q, TN) for g, q in zip(grad_s, queries)]
        for (col, head, qs, ks, slot_at), dq, dk, dv in zip(spots, dqs, dks, dvs):
            lanes = slice(head * HEAD_DIM, (head + 1) * HEAD_DIM)
            dq_win[col, qs, lanes] = dq
            dk_own[col, qs, lanes] = dk[:64]
            dv_own[col, qs, lanes] = dv[:64]
            dkv_send[col, 0, pl.ds(2 * slot_at, 2), :, lanes] = dk[64:].astype(BF16).reshape(2, TILE, HEAD_DIM)
            dkv_send[col, 1, pl.ds(2 * slot_at, 2), :, lanes] = dv[64:].astype(BF16).reshape(2, TILE, HEAD_DIM)

    def project(place):
        rows = attended[pl.ds(4 * chip_at(place), 4)].reshape(2 * OWN, WIDTH)

        def body(index, carry):
            cols = pl.ds(pl.multiple_of(index * 512, 512), 512)
            value = dot(rows, weight_ref[:, cols], NN).astype(BF16)
            parts[place, :, :, :, cols] = value.reshape(2, 2, HALF, 512)
            return carry
        lax.fori_loop(0, D // 512, body, 0)

    def add(total, other):
        def body(index, carry):
            cols = pl.ds(pl.multiple_of(index * 512, 512), 512)
            total[:, cols] = (total[:, cols].astype(F32) + other[:, cols].astype(F32)).astype(BF16)
            return carry
        lax.fori_loop(0, D // 512, body, 0)

    def part(place, half):
        return parts.at[place, core, half]

    def part_copy(place):
        return remote(parts.at[place, 1 - core], part_in.at[place], part_send.at[place],
                      part_recv.at[place], sibling)

    def partials(place):
        project(place)
        start(part_copy(place))

    def join_cores(place):
        part_copy(place).wait_recv()
        for half in range(2):
            add(part(place, half), part_in.at[place, half])

    def near_sem(place, half):
        return sum_recv.at[2 * (place - 1) + half]

    def far_sem(place, half):
        return sum_recv.at[6 + 2 * place + half]

    def send_edge(place):
        for half in range(2):
            start(remote(part(place, half), from_near.at[place - 1, half],
                         sum_send.at[2 * (place - 1) + half], near_sem(place, half), one), edge)

    def wait_near(place, half):
        ref = from_near.at[place - 1, half]
        remote(ref, ref, sum_send.at[0], near_sem(place, half), sibling).wait_recv()

    def wait_far(place, half):
        ref = from_far.at[place, half]
        remote(ref, ref, sum_send.at[0], far_sem(place, half), sibling).wait_recv()

    def pass_far(place, half):
        @pl.when(inner)
        def _():
            wait_near(place, half)
            add(part(place, half), from_near.at[place - 1, half])
        start(remote(part(place, half), from_far.at[3 - place, half],
                     sum_send.at[2 * (place - 2) + half], far_sem(3 - place, half), far), inner)

    def pass_near(half):
        @pl.when(inner)
        def _():
            wait_far(0, half)
            add(part(0, half), from_far.at[0, half])
        start(remote(part(0, half), from_far.at[0, half],
                     sum_send.at[4 + half], far_sem(0, half), near), inner)

    loads[0].wait()
    tiles = windows_ref[...]
    tile_rows = jnp.where(tiles < 2 * ROWS, tiles // 4, (tiles - 2 * ROWS) // 2)
    odd = jnp.max(tile_rows, axis=0, keepdims=True) != jnp.min(tile_rows, axis=0, keepdims=True)
    mask_ref[...] = jnp.broadcast_to(odd[:, :1].astype(F32), (TILE, WIDTH)).astype(BF16)
    mask_copy = remote(mask_ref, west_mask, mask_send.at[0], mask_recv.at[0], east)
    start(mask_copy)
    for load in loads[1:]:
        load.wait()
    own_into_windows(1)
    kv_halves[0][1]()
    kv_halves[1][0]()
    send_own(1)
    mask_copy.wait_recv()
    own_into_windows(0)
    inside = jnp.logical_not(at_end)
    gather_step(1, 0)
    kv_halves[1][1]()
    gather_step(1, 1, at_end)
    near_window = 5 + 2 * flip
    for col in (1, 0):
        kv_halves[0][2](col)
        far_into_windows(col, near_window, 3)
    forward(near_window, 3)
    attend(4 * chip_at(3), 4)
    partials(3)
    gather_step(1, 1, inside)
    join_cores(3)
    send_edge(3)
    project_order(0)
    project_order(1)
    gather_step(2, 0, at_end)
    for col in (1, 0):
        kv_halves[1][2](col)
        far_into_windows(col, near_window + 3, 5)
    forward(near_window + 3, 3)
    forward(near_window + 6, 2)
    attend(4 * chip_at(3) + 4, 12)
    gather_step(2, 0, inside)
    partials(2)
    partials(0)
    partials(1)
    join_cores(2)
    send_edge(2)
    pass_far(3, 0)
    join_cores(1)
    send_edge(1)
    join_cores(0)
    gather_step(2, 1)
    pass_far(3, 1)

    def grad_out_into_windows():
        for col in range(2):
            into_windows(col, [(lambda row, col=col: grad_out[row, col], put_query(do_win, col))])

    project_order(2)
    grad_out_into_windows()
    backward(0, 3)
    backward(3, 2)
    returns[0][0]()
    gather_step(3, 0)
    pass_near(0)
    gather_step(3, 1)
    pass_far(2, 0)
    project_order(3)
    grad_out_into_windows()
    backward(5, 3)
    early = len(pending)
    returns[1][0]()
    returns[0][1]()
    pass_near(1)
    pass_far(2, 1)
    returns[1][1]()
    for col in range(2):
        def put_dq(row, value, col=col):
            grad_ref[0, row, col] = value
        from_windows(col, [(get_window(dq_win, col), put_dq)], BF16)

    def drain(copies):
        for copy, condition in copies:
            if condition is None:
                copy.wait_send()
            else:
                pl.when(condition)(copy.wait_send)

    def add_returns(stage):
        begin, count = ((4 * flip + 1, 9), (4 * flip + 10, 7))[stage]
        for col in range(2):
            returns[stage][2](col)
            came = (dkv_west, dkv_east)[col]

            def put_sum(which, col=col):
                def write(row, value):
                    grad_ref[1 + which, row, col] = value.astype(BF16)
                return write

            def get_sum(which, ref, col=col, came=came):
                own = get_window(ref, col)
                return lambda row: own(row) + came[which, lax.rem(row + 12 * flip, ROWS)].astype(F32)

            from_windows(col, [(get_sum(0, dk_own), put_sum(0)), (get_sum(1, dv_own), put_sum(1))], F32,
                         begin, count)

    drain(pending[:early])
    add_returns(0)

    def finish(half):
        rows = pl.ds(half * HALF, HALF)

        def body(index, carry):
            cols = pl.ds(pl.multiple_of(index * 512, 512), 512)
            mixed_ref[rows, cols] = (
                parts[pos, core, half, :, cols].astype(F32)
                + from_far[pos, half, :, cols].astype(F32)
                + jnp.where(inner, from_near[0, half, :, cols].astype(F32), 0.0)
            ).astype(BF16)
            return carry
        lax.fori_loop(0, D // 512, body, 0)

    @pl.when(edge)
    def _():
        from_near[0] = jnp.zeros_like(from_near[0])
    for half in range(2):
        @pl.when(inner)
        def _():
            wait_near(1, half)
            wait_far(1, half)

        @pl.when(edge)
        def _():
            wait_far(0, half)
        finish(half)

    add_returns(1)
    drain(pending[early:])


def per_device(n_lon, qkv, windows, out_weight, cotangent):
    vmem = pl.BlockSpec(memory_space=pltpu.VMEM)
    dma = pltpu.SemaphoreType.DMA
    column = (2, ROWS, TILE, WIDTH)
    mixed, grad = pl.pallas_call(
        functools.partial(kernel, n_lon),
        out_shape=(
            jax.ShapeDtypeStruct((OWN, D), BF16),
            jax.ShapeDtypeStruct((3, ROWS, 2, TILE, WIDTH), BF16),
        ),
        in_specs=[pl.BlockSpec(memory_space=pltpu.HBM)] * 4,
        out_specs=(vmem, vmem),
        scratch_shapes=[
            pltpu.VMEM((4, WINDOWS), jnp.int32),
            pltpu.VMEM((3, ROWS, 2, TILE, WIDTH), BF16),
            pltpu.VMEM((WIDTH, D), BF16),
            pltpu.VMEM((TILE, WIDTH), BF16),
            pltpu.VMEM((TILE, WIDTH), BF16),
            pltpu.VMEM((4, 2, 2, TILE, WIDTH), BF16),
            pltpu.VMEM((4, 2, 2, TILE, WIDTH), BF16),
            pltpu.VMEM(column, BF16),
            pltpu.VMEM(column, BF16),
            pltpu.VMEM((8, 2, HALF, D), BF16),
            pltpu.VMEM((ROWS, 2, TILE, WIDTH), BF16),
            pltpu.VMEM((2, 512, WIDTH), BF16),
            pltpu.VMEM((2, 1024, WIDTH), BF16),
            pltpu.VMEM((2, 1024, WIDTH), BF16),
            pltpu.VMEM((2, 512, WIDTH), BF16),
            pltpu.VMEM((2, 2, 512, HEAD_DIM), F32),
            pltpu.VMEM((2, 512, WIDTH), BF16),
            pltpu.VMEM((ROWS, 2, TILE, WIDTH), BF16),
            pltpu.VMEM((2, 512, WIDTH), BF16),
            pltpu.VMEM((2, 512, WIDTH), F32),
            pltpu.VMEM((2, 512, WIDTH), F32),
            pltpu.VMEM((2,) + column, BF16),
            pltpu.VMEM(column, BF16),
            pltpu.VMEM(column, BF16),
            pltpu.VMEM((4, 2, 2, HALF, D), BF16),
            pltpu.VMEM((4, 2, HALF, D), BF16),
            pltpu.VMEM((3, 2, HALF, D), BF16),
            pltpu.VMEM((2, 2, HALF, D), BF16),
            dma((4,)), dma((1,)), dma((1,)), dma((4, 2, 2)), dma((4, 2, 2)), dma((4, 8)), dma((4, 8)),
            dma((4, 2)), dma((4, 2)), dma((10,)), dma((8,)), dma((8,)), dma((8,)),
            dma((4,)), dma((4,)), dma((6,)), dma((10,)),
        ],
        compiler_params=pltpu.CompilerParams(
            collective_id=0, has_side_effects=True, vmem_limit_bytes=53 * 1024 * 1024
        ),
        cost_estimate=pl.CostEstimate(
            flops=2 * 1270 * 10**6, bytes_accessed=6 * 2**20, transcendentals=2**18
        ),
    )(windows.T, qkv.reshape(3, ROWS, 2, TILE, WIDTH), out_weight, cotangent.reshape(2, HALF, D))
    return mixed, grad.reshape(3, ROWS * 2 * TILE, WIDTH)


def solution(mesh):
    in_specs = (P(None, "lon", "tp"), P("lon", None), P("tp", None), P(("lon", "tp"), None))
    out_specs = (P(("lon", "tp"), None), P(None, "lon", "tp"))
    return jax.shard_map(
        functools.partial(per_device, mesh.shape["lon"]),
        mesh=mesh, in_specs=in_specs, out_specs=out_specs, check_vma=False,
    )
```

```python
import functools

import jax
import jax.numpy as jnp
from jax import lax
from jax.experimental import pallas as pl
from jax.experimental.pallas import tpu as pltpu
from jax.sharding import PartitionSpec as P

HEAD_DIM = 128
TILE = 32
ROWS = 16
WINDOWS = 8
WIDTH = 256
D = 2048
OWN = 128
ORDER = (4, 3, 5, 2, 6, 1, 7, 0)
HALF = 64
SCALE = HEAD_DIM ** (-0.5)
MESH = pl.DeviceIdType.MESH
BF16 = jnp.bfloat16
F32 = jnp.float32

NT = (((1,), (1,)), ((), ()))
NN = (((1,), (0,)), ((), ()))
TN = (((0,), (0,)), ((), ()))


def dot(a, b, dims):
    return lax.dot_general(a, b, dims, preferred_element_type=F32)


def kernel(
    n_lon,
    windows_hbm, qkv_hbm, weight_hbm, cot_hbm,
    mixed_ref, grad_ref,
    windows_ref, qkv_ref, weight_ref, mask_ref, west_mask, relay_west, relay_east, kv_east, kv_west, gathered, grad_out, q_win, k_win, v_win, do_win,
    weights, out_win, attended, dq_win, dk_own, dv_own,
    dkv_send, dkv_east, dkv_west, parts, part_in, from_near, from_far,
    load_sem, mask_send, mask_recv, lon_send, lon_recv, piece_send, piece_recv,
    relay_send, relay_recv, tp_send, tp_recv, sib_send, sib_recv,
    part_send, part_recv, sum_send, sum_recv,
):
    lon, tp = lax.axis_index("lon"), lax.axis_index("tp")
    chip, core = tp // 2, tp % 2
    depth = lax.rem(lon, 8)
    first, last = depth == 0, depth == 7
    column_base = lon - depth
    east = {"lon": lax.rem(lon + 1, n_lon)}
    west = {"lon": lax.rem(lon + n_lon - 1, n_lon)}
    over_west = lax.rem(column_base + n_lon - 1, n_lon)
    over_east = lax.rem(column_base + 8, n_lon)
    flip = chip // 2
    pos = chip + flip * (3 - 2 * chip)
    edge, inner = pos == 0, pos == 1
    edge_chip, inner_chip = edge, inner

    def chip_at(place):
        return place + flip * (3 - 2 * place)

    def device_at(place, which):
        return 2 * chip_at(place) + which

    near = {"tp": device_at(0, core)}
    one = {"tp": device_at(1, core)}
    far = {"tp": device_at(2, core)}
    sibling = {"tp": 2 * chip + 1 - core}

    loads = [
        pltpu.make_async_copy(src, dst, load_sem.at[index])
        for index, (src, dst) in enumerate((
            (windows_hbm, windows_ref), (cot_hbm, gathered.at[tp]), (weight_hbm, weight_ref), (qkv_hbm, qkv_ref),
        ))
    ]
    for load in loads:
        load.start()

    barrier = pltpu.get_barrier_semaphore()

    def greet(target):
        pl.semaphore_signal(barrier, inc=1, device_id=target, device_id_type=MESH)

    def greet_column(base):
        def body(index, carry):
            greet({"lon": base + index})
            return carry
        lax.fori_loop(0, 8, body, 0)

    greet(sibling)
    pl.when(edge)(lambda: greet(one))

    @pl.when(inner)
    def _():
        greet(near)
        greet(far)

    @pl.when(jnp.logical_not(first))
    def _():
        greet(west)
        greet({"lon": column_base})

    @pl.when(jnp.logical_not(last))
    def _():
        greet(east)
        greet({"lon": column_base + 7})

    pl.when(first)(lambda: greet_column(over_west - 7))
    pl.when(last)(lambda: greet_column(over_east))
    at_end = jnp.logical_or(first, last)
    pl.semaphore_wait(barrier, 2 + jnp.where(inner, 1, 0) + jnp.where(at_end, 10, 4))

    def remote(src, dst, send_sem, recv_sem, target):
        return pltpu.make_async_remote_copy(
            src_ref=src, dst_ref=dst, send_sem=send_sem, recv_sem=recv_sem,
            device_id=target, device_id_type=MESH,
        )

    pending = []

    def start(copy, condition=None):
        if condition is None:
            copy.start()
        else:
            pl.when(condition)(copy.start)
        pending.append((copy, condition))

    def exchange(which, src_west, dst_east, src_east, dst_west, shares, runs):
        def rows(ref, share, place):
            return ref.at[:, pl.ds(share[2](place), share[1])]

        def direct(src, dst, side, target):
            return [
                remote(src.at[:, pl.ds(begin, length)], dst.at[:, pl.ds(begin, length)],
                       lon_send.at[which, side, run], lon_recv.at[which, side, run], target)
                for run, (begin, length) in enumerate(runs)
            ]

        direct_west = direct(src_west, dst_east, 0, west)
        direct_east = direct(src_east, dst_west, 1, east)

        sides = ((0, src_west, dst_east, relay_west, first, 0), (1, src_east, dst_west, relay_east, last, 7))

        def over(src, dst, side, condition, share, place):
            start(remote(src, rows(dst, share, place), relay_send.at[which, side],
                         piece_recv.at[which, place], {"lon": (over_west, over_east)[side]}), condition)

        def passing(relay, share):
            return relay.at[which, :, pl.ds(0, share[1])]

        def launch():
            for side, src, dst, relay, end, own_place in sides:
                for step in ORDER:
                    place = abs(own_place - step)
                    share = next((item for item in shares if place in item[0]), None)
                    if share is None:
                        continue
                    if step == 0:
                        over(rows(src, share, place), dst, side, end, share, place)
                    else:
                        start(remote(rows(src, share, place), passing(relay, share), piece_send.at[which, place],
                                     relay_recv.at[which, side], {"lon": column_base + place}), end)
            for copy in direct_west:
                start(copy, jnp.logical_not(first))
            for copy in direct_east:
                start(copy, jnp.logical_not(last))

        def forward_pieces():
            for side, src, dst, relay, end, own_place in sides:
                for share in shares:
                    among = functools.reduce(jnp.logical_or, [depth == place for place in share[0]])
                    condition = jnp.logical_and(among, jnp.logical_not(end))
                    piece = passing(relay, share)

                    @pl.when(condition)
                    def _():
                        remote(piece, piece, relay_send.at[which, side],
                               relay_recv.at[which, side], sibling).wait_recv()
                    over(piece, dst, side, condition, share, depth)

        def wait_from(side):
            copies, dst, at_column_end = ((direct_east, dst_west, first), (direct_west, dst_east, last))[side]

            @pl.when(jnp.logical_not(at_column_end))
            def _():
                for copy in copies:
                    copy.wait_recv()

            @pl.when(at_column_end)
            def _():
                for share in shares:
                    for place in share[0]:
                        ref = rows(dst, share, place)
                        remote(ref, ref, relay_send.at[which, 0], piece_recv.at[which, place], sibling).wait_recv()

        return launch, forward_pieces, wait_from

    def first_row(index):
        return jnp.where(index < 6, 10 - 10 * flip + index, 14 * flip + index - 6)

    def second_row(index):
        return 2 + 4 * flip + index

    kv_halves = [
        exchange(half, qkv_hbm.at[pl.ds(1, 2), :, 0], kv_east, qkv_hbm.at[pl.ds(1, 2), :, 1], kv_west,
                 [(range(8), 1, row_of)], runs)
        for half, (row_of, runs) in enumerate((
            (first_row, [(10 - 10 * flip, 6), (14 * flip, 2)]),
            (second_row, [(2 + 4 * flip, 8)]),
        ))
    ]
    return_shares = (
        [((0, 7), 2, lambda place: 2 * (place // 7)), (range(1, 7), 1, lambda place: 3 + place)],
        [((0, 1, 2, 5, 6, 7), 1, lambda place: 10 + place - 2 * (place // 5))],
    )
    returns = [
        exchange(2 + stage, dkv_send.at[0], dkv_east, dkv_send.at[1], dkv_west, return_shares[stage], [run])
        for stage, run in enumerate(((0, 10), (10, 6)))
    ]
    kv_halves[0][0]()

    def block(place, which, half):
        return gathered.at[device_at(place, which), half]

    def own_half(half):
        return cot_hbm.at[half]

    def slot(place, half):
        return 2 * place + half

    def send_own(half):
        start(remote(own_half(half), gathered.at[tp, half], tp_send.at[half],
                     tp_recv.at[slot(0, half)], one), edge)
        start(remote(own_half(half), gathered.at[tp, half], tp_send.at[half],
                     tp_recv.at[slot(1, half)], near), inner)
        start(remote(own_half(half), gathered.at[tp, half], tp_send.at[2 + half],
                     tp_recv.at[slot(2, half)], far), inner)
        start(remote(own_half(half), gathered.at[tp, half], sib_send.at[half],
                     sib_recv.at[half], sibling))

    send_own(0)

    def wait_tp(place, half):
        remote(block(place, core, half), block(place, core, half), tp_send.at[0],
               tp_recv.at[slot(place, half)], sibling).wait_recv()

    def hand_over(place, half, order):
        src = block(place, core, half)
        return remote(src, src, sib_send.at[2 * order + half], sib_recv.at[2 * order + half], sibling)

    def gather_step(order, half, where=None):
        def both(condition):
            return condition if where is None else jnp.logical_and(condition, where)

        edge, inner = both(edge_chip), both(inner_chip)
        if order == 1:
            @pl.when(edge)
            def _():
                wait_tp(1, half)
            start(hand_over(1, half, 1), edge)

            @pl.when(inner)
            def _():
                wait_tp(2, half)
            start(remote(block(2, core, half), block(2, core, half), tp_send.at[4 + half],
                         tp_recv.at[slot(2, half)], near), inner)
            start(hand_over(2, half, 1), inner)

            @pl.when(inner)
            def _():
                wait_tp(0, half)
            start(remote(block(0, core, half), block(0, core, half), tp_send.at[6 + half],
                         tp_recv.at[slot(3, half)], far), inner)
            start(hand_over(0, half, 2), inner)
        else:
            place = order
            if order == 2:
                @pl.when(edge)
                def _():
                    wait_tp(2, half)
                start(hand_over(2, half, 2), edge)

                @pl.when(inner)
                def _():
                    wait_tp(3, half)
                start(remote(block(3, core, half), block(3, core, half), tp_send.at[8 + half],
                             tp_recv.at[slot(3, half)], near), inner)
                start(hand_over(3, half, 3), inner)
            else:
                @pl.when(edge)
                def _():
                    wait_tp(3, half)
                start(hand_over(3, half, 3), edge)

    def place_of(order):
        return (pos, 1 + pos, 2 - 2 * pos, 3)[order]

    def wait_hand_over(order):
        for half in range(2):
            dst = gathered.at[device_at(place_of(order), 1 - core), half]
            remote(dst, dst, sib_send.at[0], sib_recv.at[2 * order + half], sibling).wait_recv()

    def project_back(order):
        source = chip_at(place_of(order))
        rows = gathered[pl.ds(2 * source, 2)].reshape(2 * OWN, D)
        value = dot(rows, weight_ref[...], NT).astype(BF16)
        grad_out[pl.ds(4 * source, 4)] = value.reshape(4, 2, TILE, WIDTH)

    def project_order(order):
        wait_hand_over(order)
        project_back(order)

    def mask_of(col):
        return (west_mask, mask_ref)[col]

    def into_windows(col, pairs, begin=0, count=ROWS):
        def body(index, carry):
            row = lax.rem(begin + index, ROWS)
            later = lax.rem(row + 1, ROWS)
            take = mask_of(col)[...] > 0
            for read, write in pairs:
                write(row, jnp.where(take, read(later), read(row)))
            return carry
        lax.fori_loop(0, count, body, 0)

    def from_windows(col, pairs, dtype, begin=0, count=ROWS):
        def body(index, carry):
            row = lax.rem(begin + index, ROWS)
            before = lax.rem(row + ROWS - 1, ROWS)
            take = mask_of(col)[...].astype(dtype) > 0
            for read, write in pairs:
                write(row, jnp.where(take, read(before), read(row)))
            return carry
        lax.fori_loop(0, count, body, 0)

    def put_query(ref, col):
        def write(row, value):
            ref[col, pl.ds(pl.multiple_of(row * TILE, TILE), TILE), :] = value
        return write

    def put_key(ref, col, remote_half):
        def write(row, value):
            window, part_of = row // 2, row % 2
            place = window * 128 + remote_half * 64 + part_of * TILE
            ref[col, pl.ds(pl.multiple_of(place, TILE), TILE), :] = value
        return write

    def get_window(ref, col):
        return lambda row: ref[col, pl.ds(pl.multiple_of(row * TILE, TILE), TILE), :]

    def own_into_windows(col):
        into_windows(col, [
            (lambda row: qkv_ref[0, row, col], put_query(q_win, col)),
            (lambda row: qkv_ref[1, row, col], put_key(k_win, col, 0)),
            (lambda row: qkv_ref[2, row, col], put_key(v_win, col, 0)),
        ])

    def far_into_windows(col, begin, count):
        kv = (kv_west, kv_east)[col]
        into_windows(col, [
            (lambda row: kv[0, row], put_key(k_win, col, 1)),
            (lambda row: kv[1, row], put_key(v_win, col, 1)),
        ], 2 * begin, 2 * count)

    UNITS = [(col, head) for col in range(2) for head in range(2)]

    def unit(ref, col, head, place):
        return ref[col, place, head * HEAD_DIM:(head + 1) * HEAD_DIM]

    def forward(begin, count):
        spots = []
        for sub in range(count):
            window = lax.rem(begin + sub, WINDOWS)
            qs = pl.ds(pl.multiple_of(window * 64, 64), 64)
            ks = pl.ds(pl.multiple_of(window * 128, 128), 128)
            spots += [(col, head, qs, ks) for col, head in UNITS]
        values = [unit(v_win, col, head, ks) for col, head, qs, ks in spots]
        scores = [
            dot(unit(q_win, col, head, qs), unit(k_win, col, head, ks), NT) * SCALE
            for col, head, qs, ks in spots
        ]
        raised = [jnp.exp(x - jnp.max(x, axis=-1, keepdims=True)) for x in scores]
        probs = [x / jnp.sum(x, axis=-1, keepdims=True) for x in raised]
        outs = [dot(x.astype(BF16), v, NN).astype(BF16) for x, v in zip(probs, values)]
        for (col, head, qs, ks), x, out in zip(spots, probs, outs):
            weights[col, head, qs, :] = x
            out_win[col, qs, head * HEAD_DIM:(head + 1) * HEAD_DIM] = out

    def attend(begin, count):
        for col in range(2):
            def put_attended(row, value, col=col):
                attended[row, col] = value
            from_windows(col, [(get_window(out_win, col), put_attended)], BF16, begin, count)

    def backward(begin, count):
        spots = []
        for sub in range(count):
            slot_at = begin + sub
            window = lax.rem(slot_at + 2 * flip, WINDOWS)
            qs = pl.ds(pl.multiple_of(window * 64, 64), 64)
            ks = pl.ds(pl.multiple_of(window * 128, 128), 128)
            spots += [(col, head, qs, ks, slot_at) for col, head in UNITS]
        queries = [unit(q_win, col, head, qs) for col, head, qs, ks, _ in spots]
        keys = [unit(k_win, col, head, ks) for col, head, qs, ks, _ in spots]
        d_outs = [unit(do_win, col, head, qs) for col, head, qs, ks, _ in spots]
        probs = [weights[col, head, qs, :] for col, head, qs, ks, _ in spots]
        grad_w = [
            dot(d, unit(v_win, col, head, ks), NT) for d, (col, head, qs, ks, _) in zip(d_outs, spots)
        ]
        dvs = [dot(x.astype(BF16), d, TN) for x, d in zip(probs, d_outs)]
        row_dots = [jnp.sum(x * g, axis=-1, keepdims=True) for x, g in zip(probs, grad_w)]
        grad_s = [(x * (g - r) * SCALE).astype(BF16) for x, g, r in zip(probs, grad_w, row_dots)]
        dqs = [dot(g, k, NN).astype(BF16) for g, k in zip(grad_s, keys)]
        dks = [dot(g, q, TN) for g, q in zip(grad_s, queries)]
        for (col, head, qs, ks, slot_at), dq, dk, dv in zip(spots, dqs, dks, dvs):
            lanes = slice(head * HEAD_DIM, (head + 1) * HEAD_DIM)
            dq_win[col, qs, lanes] = dq
            dk_own[col, qs, lanes] = dk[:64]
            dv_own[col, qs, lanes] = dv[:64]
            dkv_send[col, 0, pl.ds(2 * slot_at, 2), :, lanes] = dk[64:].astype(BF16).reshape(2, TILE, HEAD_DIM)
            dkv_send[col, 1, pl.ds(2 * slot_at, 2), :, lanes] = dv[64:].astype(BF16).reshape(2, TILE, HEAD_DIM)

    def project(place):
        rows = attended[pl.ds(4 * chip_at(place), 4)].reshape(2 * OWN, WIDTH)

        def body(index, carry):
            cols = pl.ds(pl.multiple_of(index * 512, 512), 512)
            value = dot(rows, weight_ref[:, cols], NN).astype(BF16)
            parts[place, :, :, :, cols] = value.reshape(2, 2, HALF, 512)
            return carry
        lax.fori_loop(0, D // 512, body, 0)

    def add(total, other):
        def body(index, carry):
            cols = pl.ds(pl.multiple_of(index * 512, 512), 512)
            total[:, cols] = (total[:, cols].astype(F32) + other[:, cols].astype(F32)).astype(BF16)
            return carry
        lax.fori_loop(0, D // 512, body, 0)

    def part(place, half):
        return parts.at[place, core, half]

    def part_copy(place):
        return remote(parts.at[place, 1 - core], part_in.at[place], part_send.at[place],
                      part_recv.at[place], sibling)

    def partials(place):
        project(place)
        start(part_copy(place))

    def join_cores(place):
        part_copy(place).wait_recv()
        for half in range(2):
            add(part(place, half), part_in.at[place, half])

    def near_sem(place, half):
        return sum_recv.at[2 * (place - 1) + half]

    def far_sem(place, half):
        return sum_recv.at[6 + 2 * place + half]

    def send_edge(place):
        for half in range(2):
            start(remote(part(place, half), from_near.at[place - 1, half],
                         sum_send.at[2 * (place - 1) + half], near_sem(place, half), one), edge)

    def wait_near(place, half):
        ref = from_near.at[place - 1, half]
        remote(ref, ref, sum_send.at[0], near_sem(place, half), sibling).wait_recv()

    def wait_far(place, half):
        ref = from_far.at[place, half]
        remote(ref, ref, sum_send.at[0], far_sem(place, half), sibling).wait_recv()

    def pass_far(place, half):
        @pl.when(inner)
        def _():
            wait_near(place, half)
            add(part(place, half), from_near.at[place - 1, half])
        start(remote(part(place, half), from_far.at[3 - place, half],
                     sum_send.at[2 * (place - 2) + half], far_sem(3 - place, half), far), inner)

    def pass_near(half):
        @pl.when(inner)
        def _():
            wait_far(0, half)
            add(part(0, half), from_far.at[0, half])
        start(remote(part(0, half), from_far.at[0, half],
                     sum_send.at[4 + half], far_sem(0, half), near), inner)

    loads[0].wait()
    tiles = windows_ref[...]
    tile_rows = jnp.where(tiles < 2 * ROWS, tiles // 4, (tiles - 2 * ROWS) // 2)
    odd = jnp.max(tile_rows, axis=0, keepdims=True) != jnp.min(tile_rows, axis=0, keepdims=True)
    mask_ref[...] = jnp.broadcast_to(odd[:, :1].astype(F32), (TILE, WIDTH)).astype(BF16)
    mask_copy = remote(mask_ref, west_mask, mask_send.at[0], mask_recv.at[0], east)
    start(mask_copy)
    for load in loads[1:]:
        load.wait()
    own_into_windows(1)
    kv_halves[0][1]()
    kv_halves[1][0]()
    send_own(1)
    mask_copy.wait_recv()
    own_into_windows(0)
    inside = jnp.logical_not(at_end)
    gather_step(1, 0)
    kv_halves[1][1]()
    gather_step(1, 1, at_end)
    near_window = 5 + 2 * flip
    for col in (1, 0):
        kv_halves[0][2](col)
        far_into_windows(col, near_window, 3)
    forward(near_window, 3)
    attend(4 * chip_at(3), 4)
    partials(3)
    gather_step(1, 1, inside)
    join_cores(3)
    send_edge(3)
    project_order(0)
    project_order(1)
    gather_step(2, 0, at_end)
    for col in (1, 0):
        kv_halves[1][2](col)
        far_into_windows(col, near_window + 3, 5)
    forward(near_window + 3, 3)
    forward(near_window + 6, 2)
    attend(4 * chip_at(3) + 4, 12)
    gather_step(2, 0, inside)
    partials(2)
    partials(0)
    partials(1)
    join_cores(2)
    send_edge(2)
    pass_far(3, 0)
    join_cores(1)
    send_edge(1)
    join_cores(0)
    gather_step(2, 1)

    def grad_out_into_windows():
        for col in range(2):
            into_windows(col, [(lambda row, col=col: grad_out[row, col], put_query(do_win, col))])

    project_order(2)
    grad_out_into_windows()
    backward(0, 3)
    backward(3, 2)
    returns[0][0]()
    pass_far(3, 1)
    gather_step(3, 0)
    pass_near(0)
    gather_step(3, 1)
    pass_far(2, 0)
    project_order(3)
    grad_out_into_windows()
    backward(5, 3)
    early = len(pending)
    returns[1][0]()
    returns[0][1]()
    pass_near(1)
    pass_far(2, 1)
    returns[1][1]()
    for col in range(2):
        def put_dq(row, value, col=col):
            grad_ref[0, row, col] = value
        from_windows(col, [(get_window(dq_win, col), put_dq)], BF16)

    def drain(copies):
        for copy, condition in copies:
            if condition is None:
                copy.wait_send()
            else:
                pl.when(condition)(copy.wait_send)

    def add_returns(stage):
        begin, count = ((4 * flip + 1, 9), (4 * flip + 10, 7))[stage]
        for col in range(2):
            returns[stage][2](col)
            came = (dkv_west, dkv_east)[col]

            def put_sum(which, col=col):
                def write(row, value):
                    grad_ref[1 + which, row, col] = value.astype(BF16)
                return write

            def get_sum(which, ref, col=col, came=came):
                own = get_window(ref, col)
                return lambda row: own(row) + came[which, lax.rem(row + 12 * flip, ROWS)].astype(F32)

            from_windows(col, [(get_sum(0, dk_own), put_sum(0)), (get_sum(1, dv_own), put_sum(1))], F32,
                         begin, count)

    drain(pending[:early])
    add_returns(0)

    def finish(half):
        rows = pl.ds(half * HALF, HALF)

        def body(index, carry):
            cols = pl.ds(pl.multiple_of(index * 512, 512), 512)
            mixed_ref[rows, cols] = (
                parts[pos, core, half, :, cols].astype(F32)
                + from_far[pos, half, :, cols].astype(F32)
                + jnp.where(inner, from_near[0, half, :, cols].astype(F32), 0.0)
            ).astype(BF16)
            return carry
        lax.fori_loop(0, D // 512, body, 0)

    @pl.when(edge)
    def _():
        from_near[0] = jnp.zeros_like(from_near[0])
    for half in range(2):
        @pl.when(inner)
        def _():
            wait_near(1, half)
            wait_far(1, half)

        @pl.when(edge)
        def _():
            wait_far(0, half)
        finish(half)

    add_returns(1)
    drain(pending[early:])


def per_device(n_lon, qkv, windows, out_weight, cotangent):
    vmem = pl.BlockSpec(memory_space=pltpu.VMEM)
    dma = pltpu.SemaphoreType.DMA
    column = (2, ROWS, TILE, WIDTH)
    mixed, grad = pl.pallas_call(
        functools.partial(kernel, n_lon),
        out_shape=(
            jax.ShapeDtypeStruct((OWN, D), BF16),
            jax.ShapeDtypeStruct((3, ROWS, 2, TILE, WIDTH), BF16),
        ),
        in_specs=[pl.BlockSpec(memory_space=pltpu.HBM)] * 4,
        out_specs=(vmem, vmem),
        scratch_shapes=[
            pltpu.VMEM((4, WINDOWS), jnp.int32),
            pltpu.VMEM((3, ROWS, 2, TILE, WIDTH), BF16),
            pltpu.VMEM((WIDTH, D), BF16),
            pltpu.VMEM((TILE, WIDTH), BF16),
            pltpu.VMEM((TILE, WIDTH), BF16),
            pltpu.VMEM((4, 2, 2, TILE, WIDTH), BF16),
            pltpu.VMEM((4, 2, 2, TILE, WIDTH), BF16),
            pltpu.VMEM(column, BF16),
            pltpu.VMEM(column, BF16),
            pltpu.VMEM((8, 2, HALF, D), BF16),
            pltpu.VMEM((ROWS, 2, TILE, WIDTH), BF16),
            pltpu.VMEM((2, 512, WIDTH), BF16),
            pltpu.VMEM((2, 1024, WIDTH), BF16),
            pltpu.VMEM((2, 1024, WIDTH), BF16),
            pltpu.VMEM((2, 512, WIDTH), BF16),
            pltpu.VMEM((2, 2, 512, HEAD_DIM), F32),
            pltpu.VMEM((2, 512, WIDTH), BF16),
            pltpu.VMEM((ROWS, 2, TILE, WIDTH), BF16),
            pltpu.VMEM((2, 512, WIDTH), BF16),
            pltpu.VMEM((2, 512, WIDTH), F32),
            pltpu.VMEM((2, 512, WIDTH), F32),
            pltpu.VMEM((2,) + column, BF16),
            pltpu.VMEM(column, BF16),
            pltpu.VMEM(column, BF16),
            pltpu.VMEM((4, 2, 2, HALF, D), BF16),
            pltpu.VMEM((4, 2, HALF, D), BF16),
            pltpu.VMEM((3, 2, HALF, D), BF16),
            pltpu.VMEM((2, 2, HALF, D), BF16),
            dma((4,)), dma((1,)), dma((1,)), dma((4, 2, 2)), dma((4, 2, 2)), dma((4, 8)), dma((4, 8)),
            dma((4, 2)), dma((4, 2)), dma((10,)), dma((8,)), dma((8,)), dma((8,)),
            dma((4,)), dma((4,)), dma((6,)), dma((10,)),
        ],
        compiler_params=pltpu.CompilerParams(
            collective_id=0, has_side_effects=True, vmem_limit_bytes=53 * 1024 * 1024
        ),
        cost_estimate=pl.CostEstimate(
            flops=2 * 1270 * 10**6, bytes_accessed=6 * 2**20, transcendentals=2**18
        ),
    )(windows.T, qkv.reshape(3, ROWS, 2, TILE, WIDTH), out_weight, cotangent.reshape(2, HALF, D))
    return mixed, grad.reshape(3, ROWS * 2 * TILE, WIDTH)


def solution(mesh):
    in_specs = (P(None, "lon", "tp"), P("lon", None), P("tp", None), P(("lon", "tp"), None))
    out_specs = (P(("lon", "tp"), None), P(None, "lon", "tp"))
    return jax.shard_map(
        functools.partial(per_device, mesh.shape["lon"]),
        mesh=mesh, in_specs=in_specs, out_specs=out_specs, check_vma=False,
    )
```
